512 devices in a mesh: dp: 64 (over x, z_hi, y), tensor: 8 (over z_lo, core).
Axes of the slice: x: 4, y: 4, z: 16 (z_hi: 4, z_lo: 4; z = z_hi * 4 + z_lo), core: 2. Of those that a mesh axis runs over, the one named last changes fastest.
Arguments:
- trainer_token_input: bfloat16 [16384, 8192], P('dp', 'tensor'), may hold values from -6 to 6
- cotangent: bfloat16 [16384, 1024], P('dp', 'tensor'), may hold values from -6 to 6
- adapter_a: float32 [8192, 64], P('tensor'), may hold values from -0.0625 to 0.0625
- adapter_b: float32 [64, 1024], P(None, 'tensor'), may hold values from -0.75 to 0.75
- moment_a: float32 [8192, 64], P('tensor'), may hold values from -0.06 to 0.06
- second_a: float32 [8192, 64], P('tensor'), may hold values from 1e-06 to 0.0001
- moment_b: float32 [64, 1024], P(None, 'tensor'), may hold values from -0.06 to 0.06
- second_b: float32 [64, 1024], P(None, 'tensor'), may hold values from 1e-06 to 0.0001
- value_matrix: bfloat16 [8192, 1024], P(None, 'tensor'), may hold values from -0.0625 to 0.0625
- decode_states: bfloat16 [2048, 4, 8192], P('dp', None, 'tensor'), may hold values from -6 to 6
- new_keys: bfloat16 [2048, 4, 1024], P('dp', None, 'tensor'), may hold values from -6 to 6
- queries: bfloat16 [2048, 4, 8192], P('dp', None, 'tensor')
- cache_keys: bfloat16 [2048, 32, 1024], P('dp', None, 'tensor')
- cache_values: bfloat16 [2048, 32, 1024], P('dp', None, 'tensor'), may hold values from -6 to 6
- lengths: int32 [2048], P('dp'), may hold values from 1 to 32, as said below
Outputs:
- step_a: float32 [8192, 64], P('tensor')
- step_b: float32 [64, 1024], P(None, 'tensor')
- attended: bfloat16 [2048, 4, 8192], P('dp', None, 'tensor')
The draws below stay inside these ranges and needn't reach their ends.
Inputs may be any that keep to these rules, and one draw needn't show every extreme that they name: `lengths`: the number of valid cache slots of each rollout; some rollout has all 32.
All inputs are finite; a program needn't handle non-finite values.
Results may differ from the reference program's by a relative error of at most 0.0067.
Values may be sent and summed in bfloat16 or wider, within the bound.
No kernel may reach another device: no remote copies, remote signals or barrier semaphores. Data moves between devices by JAX's collectives and lax.ppermute only.
A program may use at most 64 MiB of HBM per device.

```python
import math
import jax
import jax.numpy as jnp
from jax import lax

D = 8192
QH = 64
HD = 128
R = 64
STEPS = 4
CTX = 32
KVW = 1024
TRAINER_TOKENS = 16384
SEQS = 2048


def shared_keys(key):
    return jax.random.normal(key, (SEQS, CTX, KVW), jnp.float32)


def draw_cache_keys(key, part):
    base = shared_keys(key)
    return base.astype(jnp.bfloat16)


def draw_queries(key, part):
    key = jax.random.fold_in(key, 1)
    entries = jax.random.normal(key, (SEQS, STEPS, QH * HD), jnp.float32)
    return entries.astype(jnp.bfloat16)


def draw_lengths(key, part):
    key = jax.random.fold_in(key, 3)
    drawn = jax.random.randint(key, (SEQS,), 1, CTX + 1)
    return drawn.at[0].set(CTX).astype(jnp.int32)


def level_of(key, shape, pieces, smallest, top_value):
    def one(dim, parts):
        heights = jax.random.uniform(jax.random.fold_in(jax.random.fold_in(key, 6), dim), (parts,), jnp.float32, smallest / len(pieces), top_value / len(pieces))
        return jnp.repeat(jnp.exp(heights), shape[dim] // parts).reshape((-1,) + (1,) * (len(shape) - dim - 1))

    factor_of = one(*pieces[0])
    for cut in pieces[1:]:
        factor_of = factor_of * one(*cut)
    return factor_of


def gaussian(stream_key, dims, deviation, reach, pieces=(), kind=jnp.bfloat16):
    level = level_of(stream_key, dims, pieces, -0.22, 0.18) if pieces else 1.0
    values = jax.random.normal(stream_key, dims, jnp.float32) * deviation * level
    return jnp.minimum(jnp.maximum(values, -reach), reach).astype(kind)


def setup_inputs(seed: int = 0) -> dict:
    seeds = jax.random.split(jax.random.key(seed), 16)
    return {
        "trainer_token_input": gaussian(seeds[0], (TRAINER_TOKENS, D), 1.0, 6.0, ((0, 64), (1, 8))),
        "cotangent": gaussian(seeds[1], (TRAINER_TOKENS, KVW), 1.0, 6.0, ((0, 64), (1, 8))),
        "adapter_a": gaussian(seeds[2], (D, R), D ** -0.5, 0.0625, ((0, 8),), jnp.float32),
        "adapter_b": gaussian(seeds[3], (R, KVW), R ** -0.5, 0.75, ((1, 8),), jnp.float32),
        "moment_a": gaussian(seeds[4], (D, R), 0.01, 0.06, ((0, 8),), jnp.float32),
        "second_a": jnp.clip(jnp.exp(math.log(0.0001) - 4.6051702 * jax.random.uniform(seeds[5], (D, R), jnp.float32) ** level_of(seeds[5], (D, R), ((0, 8),), -0.2, 0.2)), 9.999999974752427e-07, 0.0001),
        "moment_b": gaussian(seeds[6], (R, KVW), 0.01, 0.06, ((1, 8),), jnp.float32),
        "second_b": jnp.clip(jnp.exp(math.log(0.0001) - 4.6051702 * jax.random.uniform(seeds[7], (R, KVW), jnp.float32) ** level_of(seeds[7], (R, KVW), ((1, 8),), -0.2, 0.2)), 9.999999974752427e-07, 0.0001),
        "value_matrix": gaussian(seeds[8], (D, KVW), D ** -0.5, 0.0625, ((1, 8),)),
        "decode_states": gaussian(seeds[9], (SEQS, STEPS, D), 1.0, 6.0, ((0, 64), (2, 8))),
        "new_keys": gaussian(seeds[10], (SEQS, STEPS, KVW), 1.0, 6.0, ((0, 64), (2, 8))),
        "queries": draw_queries(jax.random.fold_in(seeds[15], 71), 0),
        "cache_keys": draw_cache_keys(jax.random.fold_in(seeds[15], 71), 0),
        "cache_values": gaussian(seeds[13], (SEQS, CTX, KVW), 1.0, 6.0, ((0, 64), (2, 8))),
        "lengths": draw_lengths(jax.random.fold_in(seeds[15], 71), 0),
    }


adapter_scale = 2.0
learn_rate = 0.001
beta_one = 0.9
beta_two = 0.999
adam_eps = 1e-08
first_fix = 1.0 - 0.9 ** 10
second_fix = 1.0 - 0.999 ** 10

def adam_step(grad, moment, second):
    moment_new = beta_one * moment + (1.0 - beta_one) * grad
    second_new = beta_two * second + (1.0 - beta_two) * grad * grad
    return moment_new / first_fix / (jnp.sqrt(second_new / first_fix * 0.0 + second_new / second_fix) + adam_eps)

def attend(queries, cache_keys, cache_values, new_keys, new_values, lengths):
    rows, steps, width = queries.shape
    slots = cache_keys.shape[1]
    groups = cache_keys.shape[2] // HD
    heads = width // HD // groups
    keys = jnp.concatenate([cache_keys, new_keys], axis=1).reshape(rows, slots + steps, groups, HD)
    values = jnp.concatenate([cache_values, new_values], axis=1).reshape(rows, slots + steps, groups, HD)
    query = queries.reshape(rows, steps, groups, heads, HD)
    scores = jnp.einsum('sjgqd,skgd->sgqjk', query.astype(jnp.float32), keys.astype(jnp.float32)) * (1.0 / math.sqrt(HD))
    position = jnp.arange(slots + steps, dtype=jnp.int32)
    current = jnp.arange(steps, dtype=jnp.int32)
    cache_ok = (position[None, None, :] < lengths[:, None, None]) & (position[None, None, :] < slots)
    new_ok = (position[None, None, :] >= slots) & (position[None, None, :] - slots <= current[None, :, None])
    visible = (cache_ok | new_ok)[:, None, None, :, :]
    scores = jnp.where(visible, scores, -1e+30)
    largest = lax.optimization_barrier(jnp.max(scores, axis=-1, keepdims=True))
    expo = jnp.exp(scores - largest)
    weights = (expo / lax.optimization_barrier(jnp.sum(expo, axis=-1, keepdims=True))).astype(jnp.bfloat16)
    out = jnp.einsum('sgqjk,skgd->sjgqd', weights.astype(jnp.float32), values.astype(jnp.float32))
    return out.reshape(rows, steps, width).astype(jnp.bfloat16)

def reference(trainer_token_input, cotangent, adapter_a, adapter_b, moment_a, second_a, moment_b, second_b, value_matrix, decode_states, new_keys, queries, cache_keys, cache_values, lengths):
    a_low = adapter_a.astype(jnp.bfloat16)
    b_low = adapter_b.astype(jnp.bfloat16)
    low_rank_activations = jnp.dot(trainer_token_input, a_low, preferred_element_type=jnp.float32).astype(jnp.bfloat16)
    low_rank_gradients = jnp.dot(cotangent, b_low.T, preferred_element_type=jnp.float32).astype(jnp.bfloat16)
    gradient_up_matrix = jnp.dot(low_rank_activations.T, cotangent, preferred_element_type=jnp.float32) * (adapter_scale / TRAINER_TOKENS)
    gradient_down_matrix = jnp.dot(trainer_token_input.T, low_rank_gradients, preferred_element_type=jnp.float32) * (adapter_scale / TRAINER_TOKENS)
    step_a = adam_step(gradient_down_matrix, moment_a, second_a)
    step_b = adam_step(gradient_up_matrix, moment_b, second_b)
    updated_down_matrix = (adapter_a - learn_rate * step_a).astype(jnp.bfloat16)
    updated_up_matrix = (adapter_b - learn_rate * step_b).astype(jnp.bfloat16)
    merged_weight = (value_matrix.astype(jnp.float32) + adapter_scale * jnp.dot(updated_down_matrix, updated_up_matrix, preferred_element_type=jnp.float32)).astype(jnp.bfloat16)
    flat = decode_states.reshape(SEQS * STEPS, D)
    new_values = jnp.dot(flat, merged_weight, preferred_element_type=jnp.float32).astype(jnp.bfloat16).reshape(SEQS, STEPS, KVW)
    attended = attend(queries, cache_keys, cache_values, new_keys, new_values, lengths)
    return (step_a, step_b, attended)
```

```python
import math

import jax
import jax.numpy as jnp
from jax import lax
from jax.sharding import Mesh, PartitionSpec as P

HD = 128


adapter_scale = 2.0
learn_rate = 0.001
beta_one = 0.9
beta_two = 0.999
adam_eps = 1e-08
first_fix = 1.0 - 0.9**10
second_fix = 1.0 - 0.999**10

DP = ("x", "zh", "y")
PLANE = ("x", "y")
BF = jnp.bfloat16
F32 = jnp.float32


def adam_step(grad, moment, second):
    moment_new = beta_one * moment + (1.0 - beta_one) * grad
    second_new = beta_two * second + (1.0 - beta_two) * grad * grad
    return moment_new / first_fix / (jnp.sqrt(second_new / second_fix) + adam_eps)


def scatter(parts, axes):
    return lax.all_to_all(parts, axes, 0, 0, tiled=True)


def spread(value, axes):
    count = lax.axis_size(axes)
    return scatter(jnp.broadcast_to(value[None], (count,) + value.shape), axes)


def pack(rows):
    half = rows.shape[0] // 2
    return jnp.concatenate([rows[:half], rows[half:]], axis=1)


def unpack(packed):
    half = packed.shape[1] // 2
    return jnp.concatenate([packed[:, :half], packed[:, half:]], axis=0)


def local(
    trainer_token_input,
    cotangent,
    adapter_a,
    adapter_b,
    moment_a,
    second_a,
    moment_b,
    second_b,
    value_matrix,
    decode_states,
    new_keys,
    queries,
    cache_keys,
    cache_values,
    lengths,
):
    tensor = lax.axis_size("tensor")
    plane = lax.axis_size(PLANE)
    tokens, width = trainer_token_input.shape
    rank = adapter_a.shape[1]
    kv = cotangent.shape[1]
    rows, steps, _ = decode_states.shape
    count = rows * steps
    flat = decode_states.reshape(count, width)
    gathered = lax.all_gather(flat, "tensor", axis=0, tiled=False)

    acts_part = jnp.dot(trainer_token_input, adapter_a.astype(BF), preferred_element_type=F32)
    grads_part = jnp.dot(cotangent, adapter_b.astype(BF).T, preferred_element_type=F32)
    both = jnp.concatenate([acts_part, grads_part], axis=1).astype(BF)
    share = scatter(both.reshape(tensor, tokens // tensor, 2 * rank), "tensor")
    share = jnp.sum(share.astype(F32), axis=0).astype(BF)
    low = spread(share, "tensor").reshape(tokens, 2 * rank)
    acts, grads = low[:, :rank], low[:, rank:]

    scale_factor = adapter_scale / (tokens * lax.axis_size(DP))
    half = width // 2
    blank = jnp.zeros_like(grads)
    grad_a = jnp.dot(
        trainer_token_input[:, :half].T, jnp.concatenate([grads, blank], 1), preferred_element_type=F32
    ) + jnp.dot(
        trainer_token_input[:, half:].T, jnp.concatenate([blank, grads], 1), preferred_element_type=F32
    )
    grad_b = jnp.dot(acts.T, cotangent, preferred_element_type=F32)
    rows_a, rows_b = half // plane, rank // plane
    block = jnp.concatenate(
        [
            grad_a.reshape(plane, rows_a, 2 * rank),
            grad_b.reshape(plane, rows_b, kv),
            jnp.zeros((plane, -(rows_a + rows_b) % 8, kv), F32),
        ],
        axis=1,
    )
    shard = scatter((block * scale_factor).astype(BF), PLANE)
    shard = jnp.sum(shard.astype(F32), axis=0).astype(BF)
    shard = jnp.sum(spread(shard, ("zh",)).astype(F32), axis=0)

    place = lax.axis_index(PLANE)

    def piece_a(whole):
        low_rows = lax.dynamic_slice_in_dim(whole, place * rows_a, rows_a, 0)
        high_rows = lax.dynamic_slice_in_dim(whole, half + place * rows_a, rows_a, 0)
        return jnp.concatenate([low_rows, high_rows], axis=1)

    def piece_b(whole):
        return lax.dynamic_slice_in_dim(whole, place * rows_b, rows_b, 0)

    pad = jnp.ones((-(rows_a + rows_b) % 8, kv), F32)

    def piece(of_a, of_b):
        return jnp.concatenate([piece_a(of_a), piece_b(of_b), pad], axis=0)

    step = adam_step(shard, piece(moment_a, moment_b), piece(second_a, second_b)).astype(BF)
    every = spread(step, PLANE).astype(F32)
    step_a_packed = every[:, :rows_a].reshape(half, 2 * rank)
    step_b = every[:, rows_a : rows_a + rows_b].reshape(rank, kv)
    step_a = unpack(step_a_packed)
    new_a = (pack(adapter_a) - learn_rate * step_a_packed).astype(BF)
    new_b = (adapter_b - learn_rate * step_b).astype(BF)

    left = jnp.dot(flat[:, :half], new_a, preferred_element_type=F32)
    right = jnp.dot(flat[:, half:], new_a, preferred_element_type=F32)
    lane = lax.broadcasted_iota(jnp.int32, left.shape, 1)
    inner = jnp.where(lane < rank, left, right).astype(BF)
    inner = jnp.sum(spread(inner, "tensor").astype(F32), axis=0).astype(BF)
    twice = jnp.concatenate([new_b, new_b], axis=0)
    change = jnp.dot(inner, twice, preferred_element_type=F32)
    base = jnp.einsum(
        "tnd,tdk->nk", gathered, value_matrix.reshape(tensor, width, kv), preferred_element_type=F32
    )
    new_values = (base + adapter_scale * change).astype(BF)

    heads = queries.shape[2] // HD
    slots = cache_keys.shape[1]
    query = queries.reshape(rows, steps, heads, HD)
    keys = jnp.concatenate([cache_keys, new_keys], axis=1)
    scores = jnp.einsum("sjqd,skd->sqjk", query, keys, preferred_element_type=F32) * (
        1.0 / math.sqrt(HD)
    )
    position = jnp.arange(slots + steps, dtype=jnp.int32)
    current = jnp.arange(steps, dtype=jnp.int32)
    cache_ok = (position[None, None, :] < lengths[:, None, None]) & (position[None, None, :] < slots)
    new_ok = (position[None, None, :] >= slots) & (
        position[None, None, :] - slots <= current[None, :, None]
    )
    visible = (cache_ok | new_ok)[:, None, :, :]
    scores = jnp.where(visible, scores, -1e30)
    largest = jnp.max(scores, axis=-1, keepdims=True)
    expo = jnp.exp(scores - largest)
    weights = (expo / jnp.sum(expo, axis=-1, keepdims=True)).astype(BF)
    values = jnp.concatenate([cache_values, new_values.reshape(rows, steps, kv)], axis=1)
    out = jnp.einsum("sqjk,skd->sjqd", weights, values, preferred_element_type=F32)
    attended = out.reshape(rows, steps, heads * HD).astype(BF)
    return (step_a, step_b, attended)


def solution(mesh):
    fine = Mesh(mesh.devices.reshape(4, 4, 4, mesh.devices.shape[1]), DP + ("tensor",))
    return jax.shard_map(
        local,
        mesh=fine,
        in_specs=(
            P(DP, "tensor"),
            P(DP, "tensor"),
            P("tensor", None),
            P(None, "tensor"),
            P("tensor", None),
            P("tensor", None),
            P(None, "tensor"),
            P(None, "tensor"),
            P(None, "tensor"),
            P(DP, None, "tensor"),
            P(DP, None, "tensor"),
            P(DP, None, "tensor"),
            P(DP, None, "tensor"),
            P(DP, None, "tensor"),
            P(DP),
        ),
        out_specs=(P("tensor", None), P(None, "tensor"), P(DP, None, "tensor")),
        check_vma=False,
    )
```

```python
import math

import jax
import jax.numpy as jnp
from jax import lax
from jax.experimental import pallas as pl
from jax.experimental.pallas import tpu as pltpu
from jax.sharding import Mesh, PartitionSpec as P

HD = 128


adapter_scale = 2.0
learn_rate = 0.001
beta_one = 0.9
beta_two = 0.999
adam_eps = 1e-08
first_fix = 1.0 - 0.9**10
second_fix = 1.0 - 0.999**10

DP = ("x", "zh", "y")
PLANE = ("x", "y")
TENSOR = ("zl", "core")
BF = jnp.bfloat16
F32 = jnp.float32


def adam_step(grad, moment, second):
    moment_new = beta_one * moment + (1.0 - beta_one) * grad
    second_new = beta_two * second + (1.0 - beta_two) * grad * grad
    return moment_new / first_fix / (jnp.sqrt(second_new / second_fix) + adam_eps)


def trade(parts, axes):
    return lax.all_to_all(parts, axes, 0, 0, tiled=True)


def swap(value):
    return lax.ppermute(value, "core", [(0, 1), (1, 0)])


def call(body, out, *args, flops=0, moved=0, **more):
    return pl.pallas_call(
        body,
        out_shape=out,
        cost_estimate=pl.CostEstimate(flops=flops, bytes_accessed=moved, transcendentals=0),
        compiler_params=pltpu.CompilerParams(vmem_limit_bytes=32 * 2**20),
        **more,
    )(*args)


def shape(dims, kind):
    return jax.ShapeDtypeStruct(dims, kind)


def columns_dot(a, b):
    return lax.dot_general(a, b, (((0,), (0,)), ((), ())), preferred_element_type=F32)


def rows_dot(a, b):
    return lax.dot_general(a, b, (((1,), (1,)), ((), ())), preferred_element_type=F32)


def turn(value):
    half = value.shape[1] // 2
    return jnp.concatenate([value[:, half:], value[:, :half]], axis=1)


def lanes(value):
    return lax.broadcasted_iota(jnp.int32, value.shape, 1)


def low_body(x_ref, cot_ref, a_ref, b_ref, mine_ref, theirs_ref):
    acts = jnp.dot(x_ref[...], a_ref[...].astype(BF), preferred_element_type=F32)
    grads = rows_dot(cot_ref[...], b_ref[...].astype(BF))
    both = jnp.concatenate([acts, grads], axis=1)
    half = both.shape[0] // 2
    first = lax.axis_index("core") == 0
    mine_ref[...] = jnp.where(first, both[:half], both[half:])
    theirs_ref[...] = jnp.where(first, both[half:], both[:half])


def pair_body(mine_ref, theirs_ref, out_ref):
    total = (mine_ref[...] + theirs_ref[...]).astype(BF)
    for i in range(out_ref.shape[0]):
        out_ref[i] = total


def gradient_body(scale, x_ref, cot_ref, mine_ref, theirs_ref, out_ref):
    mine, theirs = mine_ref[...].astype(F32), theirs_ref[...].astype(F32)
    first = lax.axis_index("core") == 0
    low = jnp.concatenate([jnp.where(first, mine, theirs), jnp.where(first, theirs, mine)], axis=0)
    rank = low.shape[1] // 2
    upper = jnp.where(lanes(low) >= rank, low, 0.0).astype(BF)
    lower = jnp.where(lanes(low) < rank, turn(low), 0.0).astype(BF)
    half = x_ref.shape[1] // 2
    grad_a = (columns_dot(x_ref[:, :half], lower) + columns_dot(x_ref[:, half:], upper)) * scale
    grad_b = columns_dot(low.astype(BF), cot_ref[...])[:rank] * scale
    count, deep, wide = out_ref.shape
    rows_a, rows_b = half // count, rank // count
    blank = jnp.zeros((deep - rows_a - rows_b, wide), F32)
    for i in range(count):
        parts = [grad_a[i * rows_a : (i + 1) * rows_a], grad_b[i * rows_b : (i + 1) * rows_b], blank]
        out_ref[i] = jnp.concatenate(parts, axis=0).astype(BF)


def total_of(ref):
    total = ref[0].astype(F32)
    for i in range(1, ref.shape[0]):
        total = total + ref[i].astype(F32)
    return total


def sum_body(in_ref, out_ref):
    total = total_of(in_ref)
    for i in range(out_ref.shape[0]):
        out_ref[i] = total


def adam_body(in_ref, moment_ref, second_ref, out_ref):
    step = adam_step(total_of(in_ref), moment_ref[...], second_ref[...]).astype(BF)
    for i in range(out_ref.shape[0]):
        out_ref[i] = step


def inner_body(step_ref, a_ref, flat_ref, out_ref):
    count = step_ref.shape[0]
    half = a_ref.shape[0]
    rows_a = half // count
    step = jnp.concatenate([step_ref[i][:rows_a].astype(F32) for i in range(count)], axis=0)
    new_a = (a_ref[...] - learn_rate * step).astype(BF)
    left = jnp.dot(flat_ref[:, :half], new_a, preferred_element_type=F32)
    right = jnp.dot(flat_ref[:, half:], new_a, preferred_element_type=F32)
    inner = left + turn(right)
    top = inner.shape[0] // 2
    inner = jnp.where(lanes(inner[:top]) < inner.shape[1] // 2, inner[:top], turn(inner[top:]))
    inner = inner.astype(BF)
    for i in range(out_ref.shape[0]):
        out_ref[i] = inner


def base_body(mine_ref, theirs_ref, *refs):
    *near, far_ref, value_ref, out_ref = refs
    core, chip = lax.axis_index("core"), lax.axis_index("zl")
    pairs = value_ref.shape[0]
    total = jnp.dot(mine_ref[...], value_ref[chip, core], preferred_element_type=F32)
    total += jnp.dot(theirs_ref[...], value_ref[chip, 1 - core], preferred_element_type=F32)
    for i in range(1, pairs):
        place = lax.rem(chip + (pairs - i), pairs)
        total += jnp.dot(near[i - 1][...], value_ref[place, core], preferred_element_type=F32)
        total += jnp.dot(far_ref[i - 1], value_ref[place, 1 - core], preferred_element_type=F32)
    out_ref[...] = total


def cache_body(steps, q_ref, k_ref, v_ref, new_ref, length_ref, out_ref, weight_ref):
    groups, wide = length_ref.shape
    tall = q_ref.shape[0] // groups
    heads = q_ref.shape[1] // HD
    slots = wide // (tall // steps)
    row = lax.broadcasted_iota(jnp.int32, (heads * tall, wide), 0) % tall
    column = lax.broadcasted_iota(jnp.int32, (heads * tall, wide), 1)
    same = row // steps == column // slots
    slot = column % slots
    scale = 1.0 / math.sqrt(HD)
    for g in range(groups):
        query = jnp.concatenate(
            [q_ref[g * tall : (g + 1) * tall, h * HD : (h + 1) * HD] for h in range(heads)], axis=0
        )
        old = rows_dot(query, k_ref[g * wide : (g + 1) * wide, :]) * scale
        old = jnp.where(same & (slot < length_ref[g : g + 1, :]), old, -1e30)
        new = rows_dot(query, new_ref[...]) * scale
        token = column - g * tall
        seen = (token >= 0) & (token < tall) & (token // steps == row // steps) & (token <= row)
        new = jnp.where(seen, new, -1e30)
        largest = jnp.maximum(
            jnp.max(old, axis=1, keepdims=True), jnp.max(new, axis=1, keepdims=True)
        )
        old, new = jnp.exp(old - largest), jnp.exp(new - largest)
        total = jnp.sum(old, axis=1, keepdims=True) + jnp.sum(new, axis=1, keepdims=True)
        at = slice(g * heads * tall, (g + 1) * heads * tall)
        weight_ref[at, :] = (new / total).astype(BF)
        out_ref[at, :] = jnp.dot(
            (old / total).astype(BF), v_ref[g * wide : (g + 1) * wide, :], preferred_element_type=F32
        )


def last_body(groups, inner_ref, twice_ref, base_ref, old_ref, weight_ref, out_ref):
    inner = total_of(inner_ref).astype(BF).astype(F32)
    rank = inner.shape[1] // 2
    lower = jnp.where(lanes(inner) < rank, inner, 0.0)
    upper = jnp.where(lanes(inner) >= rank, inner, 0.0)
    both = jnp.concatenate([lower, upper], axis=0).astype(BF)
    change = jnp.dot(both, twice_ref[...], preferred_element_type=F32)
    values = (base_ref[...] + adapter_scale * change).astype(BF)
    tall = out_ref.shape[0] // groups
    heads = out_ref.shape[1] // HD
    for g in range(groups):
        at = slice(g * heads * tall, (g + 1) * heads * tall)
        out = old_ref[at, :] + jnp.dot(weight_ref[at, :], values, preferred_element_type=F32)
        out = out.astype(BF)
        for h in range(heads):
            out_ref[g * tall : (g + 1) * tall, h * HD : (h + 1) * HD] = out[h * tall : (h + 1) * tall]


def local(
    trainer_token_input,
    cotangent,
    adapter_a,
    adapter_b,
    moment_a,
    second_a,
    moment_b,
    second_b,
    value_matrix,
    decode_states,
    new_keys,
    queries,
    cache_keys,
    cache_values,
    lengths,
):
    pairs = lax.axis_size("zl")
    tensor = lax.axis_size(TENSOR)
    plane = lax.axis_size(PLANE)
    tokens, width = trainer_token_input.shape
    rank = adapter_a.shape[1]
    kv = cotangent.shape[1]
    rows, steps, _ = decode_states.shape
    count = rows * steps
    slots = cache_keys.shape[1]
    half = width // 2
    two = 2 * rank
    flat = decode_states.reshape(count, width)

    mine, theirs = call(
        low_body,
        (shape((tokens // 2, two), F32), shape((tokens // 2, two), F32)),
        trainer_token_input,
        cotangent,
        adapter_a,
        adapter_b,
    )
    pair = call(pair_body, shape((pairs, tokens // 2, two), BF), mine, swap(theirs))
    mine = jnp.sum(trade(pair, "zl").astype(F32), axis=0).astype(BF)
    theirs = swap(mine)

    rows_a, rows_b = half // plane, rank // plane
    deep = rows_a + rows_b + -(rows_a + rows_b) % 16
    scale = adapter_scale / (tokens * lax.axis_size(DP))
    block = call(
        lambda *refs: gradient_body(scale, *refs),
        shape((plane, deep, two), BF),
        trainer_token_input,
        cotangent,
        mine,
        theirs,
    )

    block, send = lax.optimization_barrier((block, flat))
    shard = trade(block, PLANE)
    near = [
        lax.ppermute(send, "zl", [(i, (i + hop) % pairs) for i in range(pairs)])
        for hop in range(1, pairs)
    ]

    shard = call(sum_body, shape((lax.axis_size("zh"), deep, two), F32), shard)
    shard = trade(shard, "zh")
    shard, near = lax.optimization_barrier((shard, near))

    place = lax.axis_index(PLANE)

    def piece(of_a, of_b):
        low_rows = lax.dynamic_slice_in_dim(of_a, place * rows_a, rows_a, 0)
        high_rows = lax.dynamic_slice_in_dim(of_a, half + place * rows_a, rows_a, 0)
        b_rows = lax.dynamic_slice_in_dim(of_b, place * rows_b, rows_b, 0)
        pad = jnp.ones((deep - rows_a - rows_b, kv), F32)
        return jnp.concatenate([jnp.concatenate([low_rows, high_rows], axis=1), b_rows, pad], axis=0)

    step = call(
        adam_body,
        shape((plane, deep, two), BF),
        shard,
        piece(moment_a, moment_b),
        piece(second_a, second_b),
    )
    step = trade(step, PLANE)

    inner = call(
        inner_body,
        shape((tensor, count // 2, two), BF),
        step,
        jnp.concatenate([adapter_a[:half], adapter_a[half:]], axis=1),
        flat,
    )
    inner = trade(inner, TENSOR)

    step_a = step[:, :rows_a].astype(F32).reshape(half, two)
    step_a = jnp.concatenate([step_a[:, :rank], step_a[:, rank:]], axis=0)
    step_b = step[:, rows_a : rows_a + rows_b].astype(F32).reshape(rank, kv)
    new_b = (adapter_b - learn_rate * step_b).astype(BF)
    twice = jnp.concatenate([new_b, new_b], axis=0)

    far = swap(jnp.stack(near))
    base = call(
        base_body,
        shape((count, kv), F32),
        flat,
        swap(flat),
        *near,
        far,
        value_matrix.reshape(pairs, 2, width, kv),
        flops=2 * count * tensor * width * kv,
        moved=8 * 2**20,
    )

    groups = rows * slots // HD
    heads = queries.shape[2] // HD
    old, weights = call(
        lambda *refs: cache_body(steps, *refs),
        (shape((count * heads, HD), F32), shape((count * heads, count), BF)),
        queries.reshape(count, heads * HD),
        cache_keys.reshape(rows * slots, kv),
        cache_values.reshape(rows * slots, kv),
        new_keys.reshape(count, kv),
        jnp.repeat(lengths, slots).reshape(groups, HD),
        flops=2 * count * heads * HD * HD * 3,
        moved=8 * 2**20,
    )
    attended = call(
        lambda *refs: last_body(groups, *refs),
        shape((count, heads * HD), BF),
        inner,
        twice,
        base,
        old,
        weights,
    )
    return (step_a, step_b, attended.reshape(rows, steps, heads * HD))


def solution(mesh):
    sizes = (4, 4, 4, mesh.devices.shape[1] // 2, 2)
    fine = Mesh(mesh.devices.reshape(sizes), DP + TENSOR)
    return jax.shard_map(
        local,
        mesh=fine,
        in_specs=(
            P(DP, TENSOR),
            P(DP, TENSOR),
            P(TENSOR, None),
            P(None, TENSOR),
            P(TENSOR, None),
            P(TENSOR, None),
            P(None, TENSOR),
            P(None, TENSOR),
            P(None, TENSOR),
            P(DP, None, TENSOR),
            P(DP, None, TENSOR),
            P(DP, None, TENSOR),
            P(DP, None, TENSOR),
            P(DP, None, TENSOR),
            P(DP),
        ),
        out_specs=(P(TENSOR, None), P(None, TENSOR), P(DP, None, TENSOR)),
        check_vma=False,
    )
```

```python
import math

import jax
import jax.numpy as jnp
from jax import lax
from jax.experimental import pallas as pl
from jax.experimental.pallas import tpu as pltpu
from jax.sharding import Mesh, PartitionSpec as P

HD = 128


adapter_scale = 2.0
learn_rate = 0.001
beta_one = 0.9
beta_two = 0.999
adam_eps = 1e-08
first_fix = 1.0 - 0.9**10
second_fix = 1.0 - 0.999**10

DP = ("x", "zh", "y")
PLANE = ("x", "y")
TENSOR = ("zl", "core")
BF = jnp.bfloat16
F32 = jnp.float32


def adam_step(grad, moment, second):
    moment_new = beta_one * moment + (1.0 - beta_one) * grad
    second_new = beta_two * second + (1.0 - beta_two) * grad * grad
    return moment_new / first_fix / (jnp.sqrt(second_new / second_fix) + adam_eps)


def trade(parts, axes):
    return lax.all_to_all(parts, axes, 0, 0, tiled=True)


def swap(value):
    return lax.ppermute(value, "core", [(0, 1), (1, 0)])


def reach(value, hop):
    return lax.ppermute(value, "zl", [(i, i ^ hop) for i in range(lax.axis_size("zl"))])


def call(body, out, *args, flops=0, moved=0, **more):
    return pl.pallas_call(
        body,
        out_shape=out,
        cost_estimate=pl.CostEstimate(flops=flops, bytes_accessed=moved, transcendentals=0),
        compiler_params=pltpu.CompilerParams(vmem_limit_bytes=16 * 2**20),
        **more,
    )(*args)


def far(value):
    return pltpu.with_memory_space_constraint(value, pltpu.HBM)


def shape(dims, kind):
    return jax.ShapeDtypeStruct(dims, kind)


def columns_dot(a, b):
    return lax.dot_general(a, b, (((0,), (0,)), ((), ())), preferred_element_type=F32)


def rows_dot(a, b):
    return lax.dot_general(a, b, (((1,), (1,)), ((), ())), preferred_element_type=F32)


def low_body(x_ref, cot_ref, a_ref, b_ref, mine_ref, theirs_ref):
    acts = rows_dot(x_ref[...], a_ref[...].astype(BF))
    grads = rows_dot(cot_ref[...], b_ref[...].astype(BF))
    both = jnp.concatenate([acts, grads], axis=1)
    half = both.shape[0] // 2
    first = lax.axis_index("core") == 0
    mine_ref[...] = jnp.where(first, both[:half], both[half:])
    theirs_ref[...] = jnp.where(first, both[half:], both[:half])


def pair_body(mine_ref, theirs_ref, out_ref):
    total = (mine_ref[...] + theirs_ref[...]).astype(BF)
    for i in range(out_ref.shape[0]):
        out_ref[i] = total


def stack(value, wide):
    return jnp.concatenate([value[:, i : i + wide] for i in range(0, value.shape[1], wide)], axis=0)


def unstack(value, tall):
    return jnp.concatenate([value[i : i + tall] for i in range(0, value.shape[0], tall)], axis=1)


def gradient_body(scale, x_ref, cot_ref, mine_ref, theirs_ref, out_ref):
    mine, theirs = mine_ref[...].astype(F32), theirs_ref[...].astype(F32)
    first = lax.axis_index("core") == 0
    low = jnp.concatenate([jnp.where(first, mine, theirs), jnp.where(first, theirs, mine)], axis=0)
    rank = low.shape[1] // 2
    low = low.astype(BF)
    count, deep, wide = out_ref.shape
    grad_a = stack(columns_dot(low, x_ref[...])[rank:], wide) * scale
    grad_b = columns_dot(low, cot_ref[...])[:rank] * scale
    rows_a, rows_b = grad_a.shape[0] // count, rank // count
    blank = jnp.zeros((deep - rows_a - rows_b, wide), F32)
    for i in range(count):
        parts = [grad_a[i * rows_a : (i + 1) * rows_a], grad_b[i * rows_b : (i + 1) * rows_b], blank]
        out_ref[i] = jnp.concatenate(parts, axis=0).astype(BF)


def total_of(ref):
    total = ref[0].astype(F32)
    for i in range(1, ref.shape[0]):
        total = total + ref[i].astype(F32)
    return total


def sum_body(in_ref, out_ref):
    total = total_of(in_ref)
    for i in range(out_ref.shape[0]):
        out_ref[i] = total


def shard_body(moment_a_ref, second_a_ref, moment_b_ref, second_b_ref, moment_ref, second_ref):
    deep, wide = moment_ref.shape
    rank = moment_a_ref.shape[0]
    count = lax.axis_size(PLANE)
    rows_a, rows_b = rank * moment_a_ref.shape[1] // wide // count, rank // count
    place = lax.axis_index(PLANE)
    column = pl.multiple_of(place * rows_a // rank * wide, wide)
    row = pl.multiple_of(lax.rem(place * rows_a, rank), rows_a)
    most = max(rows_b, 8)
    row_b = pl.multiple_of(place * rows_b // most * most, most)

    def piece(a_ref, b_ref):
        of_b = b_ref[pl.ds(row_b, most), :]
        chosen = of_b[:rows_b]
        for i in range(rows_b, most, rows_b):
            chosen = jnp.where(place * rows_b == row_b + i, of_b[i : i + rows_b], chosen)
        pad = jnp.ones((deep - rows_a - rows_b, wide), F32)
        return jnp.concatenate([a_ref[pl.ds(row, rows_a), pl.ds(column, wide)], chosen, pad], axis=0)

    moment_ref[...] = piece(moment_a_ref, moment_b_ref)
    second_ref[...] = piece(second_a_ref, second_b_ref)


def adam_body(in_ref, moment_ref, second_ref, out_ref):
    step = adam_step(total_of(in_ref), moment_ref[...], second_ref[...]).astype(BF)
    for i in range(out_ref.shape[0]):
        out_ref[i] = step


def step_of_a(step_ref, rank, width):
    count, _, wide = step_ref.shape
    rows_a = rank * width // wide // count
    step = jnp.concatenate([step_ref[i].astype(F32)[:rows_a] for i in range(count)], axis=0)
    return unstack(step, rank)


def inner_body(step_ref, a_ref, flat_ref, out_ref):
    rank, width = a_ref.shape
    new_a = (a_ref[...] - learn_rate * step_of_a(step_ref, rank, width)).astype(BF)
    inner = rows_dot(new_a, flat_ref[...]).astype(BF)
    for i in range(out_ref.shape[0]):
        out_ref[i] = inner


def step_body(step_ref, b_ref, step_a_ref, step_b_ref, new_b_ref):
    count = step_ref.shape[0]
    rank, width = step_a_ref.shape
    rows_a, rows_b = rank * width // step_ref.shape[2] // count, rank // count
    step_a_ref[...] = step_of_a(step_ref, rank, width)
    parts = [step_ref[i].astype(F32)[rows_a : rows_a + rows_b] for i in range(count)]
    step_b = jnp.concatenate(parts, axis=0)
    step_b_ref[...] = step_b
    new_b_ref[...] = (b_ref[...] - learn_rate * step_b).astype(BF)


def base_body(value_ref, *refs):
    pieces, out_ref, held, value, copied = refs[:4], *refs[4:]
    core, chip = lax.axis_index("core"), lax.axis_index("zl")
    chips = value.shape[0]
    half = chips // 2
    copies = []
    for i in range(chips):
        place = lax.bitwise_xor(chip, i)
        for j in range(2):
            copies.append(
                (
                    pltpu.make_async_copy(
                        pieces[2 * j + i // half].at[i % half], held.at[i, j], copied.at[i, j, 0]
                    ),
                    pltpu.make_async_copy(
                        value_ref.at[place, core if j == 0 else 1 - core], value.at[i, j], copied.at[i, j, 1]
                    ),
                )
            )
    for pair in copies:
        for copy in pair:
            copy.start()
    total = jnp.zeros(out_ref.shape, F32)
    for i in range(chips):
        for j in range(2):
            for copy in copies[2 * i + j]:
                copy.wait()
            total += jnp.dot(held[i, j], value[i, j], preferred_element_type=F32)
    out_ref[...] = total


def cache_body(steps, q_ref, k_ref, v_ref, new_ref, length_ref, out_ref, weight_ref):
    groups, wide = length_ref.shape
    tall = q_ref.shape[0] // groups
    heads = q_ref.shape[1] // HD
    slots = wide // (tall // steps)
    row = lax.broadcasted_iota(jnp.int32, (heads * tall, wide), 0) % tall
    column = lax.broadcasted_iota(jnp.int32, (heads * tall, wide), 1)
    same = row // steps == column // slots
    slot = column % slots
    scale = 1.0 / math.sqrt(HD)
    for g in range(groups):
        query = jnp.concatenate(
            [q_ref[g * tall : (g + 1) * tall, h * HD : (h + 1) * HD] for h in range(heads)], axis=0
        )
        old = rows_dot(query, k_ref[g * wide : (g + 1) * wide, :]) * scale
        old = jnp.where(same & (slot < length_ref[g : g + 1, :]), old, -1e30)
        new = rows_dot(query, new_ref[...]) * scale
        token = column - g * tall
        seen = (token >= 0) & (token < tall) & (token // steps == row // steps) & (token <= row)
        new = jnp.where(seen, new, -1e30)
        largest = jnp.maximum(
            jnp.max(old, axis=1, keepdims=True), jnp.max(new, axis=1, keepdims=True)
        )
        old, new = jnp.exp(old - largest), jnp.exp(new - largest)
        total = jnp.sum(old, axis=1, keepdims=True) + jnp.sum(new, axis=1, keepdims=True)
        at = slice(g * heads * tall, (g + 1) * heads * tall)
        weight_ref[at, :] = (new / total).astype(BF)
        out_ref[at, :] = jnp.dot(
            (old / total).astype(BF), v_ref[g * wide : (g + 1) * wide, :], preferred_element_type=F32
        )


def last_body(groups, inner_ref, new_b_ref, base_ref, old_ref, weight_ref, out_ref):
    inner = total_of(inner_ref).astype(BF)
    change = columns_dot(inner, new_b_ref[...])
    values = (base_ref[...] + adapter_scale * change).astype(BF)
    rows, steps, wide = out_ref.shape
    each = rows // groups
    tall = each * steps
    heads = wide // HD
    for g in range(groups):
        at = slice(g * heads * tall, (g + 1) * heads * tall)
        out = old_ref[at, :] + jnp.dot(weight_ref[at, :], values, preferred_element_type=F32)
        for h in range(heads):
            part = out[h * tall : (h + 1) * tall].reshape(each, steps, HD)
            out_ref[g * each : (g + 1) * each, :, h * HD : (h + 1) * HD] = part.astype(BF)


def local(
    trainer_token_input,
    cotangent,
    adapter_a,
    adapter_b,
    moment_a,
    second_a,
    moment_b,
    second_b,
    value_matrix,
    decode_states,
    new_keys,
    queries,
    cache_keys,
    cache_values,
    lengths,
):
    pairs = lax.axis_size("zl")
    tensor = lax.axis_size(TENSOR)
    plane = lax.axis_size(PLANE)
    tokens, width = trainer_token_input.shape
    rank = adapter_a.shape[1]
    kv = cotangent.shape[1]
    rows, steps, _ = decode_states.shape
    count = rows * steps
    slots = cache_keys.shape[1]
    two = 2 * rank
    flat = decode_states.reshape(count, width)
    a_turned = adapter_a.T

    half = shape((tokens // 2, two), F32)
    starts = (trainer_token_input, cotangent, a_turned, adapter_b)
    mine, theirs = call(low_body, (half, half), *map(far, starts))
    pair = call(pair_body, shape((pairs, tokens // 2, two), BF), mine, swap(theirs))

    pair, send = lax.optimization_barrier((pair, flat))
    next_chip = reach(send[None], 1)
    mine = jnp.sum(trade(pair, "zl").astype(F32), axis=0).astype(BF)
    theirs = swap(mine)

    rows_a, rows_b = rank * width // kv // plane, rank // plane
    deep = rows_a + rows_b + -(rows_a + rows_b) % 16
    scale = adapter_scale / (tokens * lax.axis_size(DP))
    block = call(
        lambda *refs: gradient_body(scale, *refs),
        shape((plane, deep, kv), BF),
        trainer_token_input,
        cotangent,
        mine,
        theirs,
    )

    block, mine_chip, next_chip = lax.optimization_barrier((block, flat[None], next_chip))
    near = jnp.concatenate([mine_chip, next_chip], axis=0)
    distant = reach(near, 2)
    shard = trade(block, PLANE)
    shard = call(sum_body, shape((lax.axis_size("zh"), deep, kv), F32), shard)
    shard, near_sent, moments = lax.optimization_barrier(
        (shard, near, (moment_a.T, second_a.T, moment_b, second_b))
    )
    shard = trade(shard, "zh")
    near_other = swap(near_sent)
    piece = shape((deep, kv), F32)
    moments = call(shard_body, (piece, piece), *map(far, moments))
    step = call(adam_body, shape((plane, deep, kv), BF), shard, *moments)
    step, distant, near_other, query = lax.optimization_barrier((step, distant, near_other, queries))
    step = trade(step, PLANE)
    distant_other = swap(distant)
    groups = rows * slots // HD
    heads = queries.shape[2] // HD
    old, weights = call(
        lambda *refs: cache_body(steps, *refs),
        (shape((count * heads, HD), F32), shape((count * heads, count), BF)),
        query.reshape(count, heads * HD),
        far(cache_keys.reshape(rows * slots, kv)),
        far(cache_values.reshape(rows * slots, kv)),
        new_keys.reshape(count, kv),
        jnp.repeat(lengths, slots).reshape(groups, HD),
        flops=2 * count * heads * HD * HD * 3,
        moved=8 * 2**20,
    )
    step, distant_other, old, weights = lax.optimization_barrier((step, distant_other, old, weights))

    inner = call(inner_body, shape((tensor, rank, count), BF), step, a_turned, flat)
    inner = trade(inner, TENSOR)
    step_a, step_b, new_b = call(
        step_body, (shape((rank, width), F32), shape((rank, kv), F32), shape((rank, kv), BF)), step, adapter_b
    )
    base = call(
        base_body,
        shape((count, kv), F32),
        *map(far, (value_matrix.reshape(pairs, 2, width, kv), near, distant, near_other, distant_other)),
        flops=2 * count * tensor * width * kv,
        moved=4 * 2**20,
        in_specs=[pl.BlockSpec(memory_space=pl.ANY)] * 5,
        scratch_shapes=[
            pltpu.VMEM((pairs, 2, count, width), BF),
            pltpu.VMEM((pairs, 2, width, kv), BF),
            pltpu.SemaphoreType.DMA((pairs, 2, 2)),
        ],
    )

    attended = call(
        lambda *refs: last_body(groups, *refs),
        shape((rows, steps, heads * HD), BF),
        inner,
        new_b,
        base,
        old,
        weights,
    )
    return (step_a.T, step_b, attended)


def solution(mesh):
    sizes = (4, 4, 4, mesh.devices.shape[1] // 2, 2)
    fine = Mesh(mesh.devices.reshape(sizes), DP + TENSOR)
    return jax.shard_map(
        local,
        mesh=fine,
        in_specs=(
            P(DP, TENSOR),
            P(DP, TENSOR),
            P(TENSOR, None),
            P(None, TENSOR),
            P(TENSOR, None),
            P(TENSOR, None),
            P(None, TENSOR),
            P(None, TENSOR),
            P(None, TENSOR),
            P(DP, None, TENSOR),
            P(DP, None, TENSOR),
            P(DP, None, TENSOR),
            P(DP, None, TENSOR),
            P(DP, None, TENSOR),
            P(DP),
        ),
        out_specs=(P(TENSOR, None), P(None, TENSOR), P(DP, None, TENSOR)),
        check_vma=False,
    )
```

```python
import math

import jax
import jax.numpy as jnp
from jax import lax
from jax.experimental import pallas as pl
from jax.experimental.pallas import tpu as pltpu
from jax.sharding import Mesh, PartitionSpec as P

HD = 128


adapter_scale = 2.0
learn_rate = 0.001
beta_one = 0.9
beta_two = 0.999
adam_eps = 1e-08
first_fix = 1.0 - 0.9**10
second_fix = 1.0 - 0.999**10

DP = ("x", "zh", "y")
PLANE = ("x", "y")
TENSOR = ("zl", "core")
BF = jnp.bfloat16
F32 = jnp.float32


def adam_step(grad, moment, second):
    moment_new = beta_one * moment + (1.0 - beta_one) * grad
    second_new = beta_two * second + (1.0 - beta_two) * grad * grad
    return moment_new / first_fix / (jnp.sqrt(second_new / second_fix) + adam_eps)


def trade(parts, axes):
    return lax.all_to_all(parts, axes, 0, 0, tiled=True)


def swap(value):
    return lax.ppermute(value, "core", [(0, 1), (1, 0)])


def reach(value, hop):
    return lax.ppermute(value, "zl", [(i, i ^ hop) for i in range(lax.axis_size("zl"))])


def call(body, out, *args, flops=0, moved=0, **more):
    return pl.pallas_call(
        body,
        out_shape=out,
        cost_estimate=pl.CostEstimate(flops=flops, bytes_accessed=moved, transcendentals=0),
        compiler_params=pltpu.CompilerParams(vmem_limit_bytes=16 * 2**20),
        **more,
    )(*args)


def far(value):
    return pltpu.with_memory_space_constraint(value, pltpu.HBM)


def shape(dims, kind):
    return jax.ShapeDtypeStruct(dims, kind)


def columns_dot(a, b):
    return lax.dot_general(a, b, (((0,), (0,)), ((), ())), preferred_element_type=F32)


def rows_dot(a, b):
    return lax.dot_general(a, b, (((1,), (1,)), ((), ())), preferred_element_type=F32)


def low_body(x_ref, cot_ref, a_ref, b_ref, mine_ref, theirs_ref):
    acts = rows_dot(x_ref[...], a_ref[...].astype(BF))
    grads = rows_dot(cot_ref[...], b_ref[...].astype(BF))
    both = jnp.concatenate([acts, grads], axis=1)
    half = both.shape[0] // 2
    first = lax.axis_index("core") == 0
    mine_ref[...] = jnp.where(first, both[:half], both[half:])
    theirs_ref[...] = jnp.where(first, both[half:], both[:half])


def pair_body(mine_ref, theirs_ref, out_ref):
    total = (mine_ref[...] + theirs_ref[...]).astype(BF)
    for i in range(out_ref.shape[0]):
        out_ref[i] = total


def stack(value, wide):
    return jnp.concatenate([value[:, i : i + wide] for i in range(0, value.shape[1], wide)], axis=0)


def unstack(value, tall):
    return jnp.concatenate([value[i : i + tall] for i in range(0, value.shape[0], tall)], axis=1)


def gradient_body(scale, x_ref, cot_ref, mine_ref, theirs_ref, out_ref):
    mine, theirs = mine_ref[...].astype(F32), theirs_ref[...].astype(F32)
    first = lax.axis_index("core") == 0
    low = jnp.concatenate([jnp.where(first, mine, theirs), jnp.where(first, theirs, mine)], axis=0)
    rank = low.shape[1] // 2
    low = low.astype(BF)
    count, deep, wide = out_ref.shape
    grad_a = stack(columns_dot(low, x_ref[...])[rank:], wide) * scale
    grad_b = columns_dot(low, cot_ref[...])[:rank] * scale
    rows_a, rows_b = grad_a.shape[0] // count, rank // count
    blank = jnp.zeros((deep - rows_a - rows_b, wide), F32)
    for i in range(count):
        parts = [grad_a[i * rows_a : (i + 1) * rows_a], grad_b[i * rows_b : (i + 1) * rows_b], blank]
        out_ref[i] = jnp.concatenate(parts, axis=0).astype(BF)


def total_of(ref):
    total = ref[0].astype(F32)
    for i in range(1, ref.shape[0]):
        total = total + ref[i].astype(F32)
    return total


def sum_body(in_ref, out_ref):
    total = total_of(in_ref)
    for i in range(out_ref.shape[0]):
        out_ref[i] = total


def shard_body(moment_a_ref, second_a_ref, moment_b_ref, second_b_ref, moment_ref, second_ref):
    deep, wide = moment_ref.shape
    rank = moment_a_ref.shape[0]
    count = lax.axis_size(PLANE)
    rows_a, rows_b = rank * moment_a_ref.shape[1] // wide // count, rank // count
    place = lax.axis_index(PLANE)
    column = pl.multiple_of(place * rows_a // rank * wide, wide)
    row = pl.multiple_of(lax.rem(place * rows_a, rank), rows_a)
    most = max(rows_b, 8)
    row_b = pl.multiple_of(place * rows_b // most * most, most)

    def piece(a_ref, b_ref):
        of_b = b_ref[pl.ds(row_b, most), :]
        chosen = of_b[:rows_b]
        for i in range(rows_b, most, rows_b):
            chosen = jnp.where(place * rows_b == row_b + i, of_b[i : i + rows_b], chosen)
        pad = jnp.ones((deep - rows_a - rows_b, wide), F32)
        return jnp.concatenate([a_ref[pl.ds(row, rows_a), pl.ds(column, wide)], chosen, pad], axis=0)

    moment_ref[...] = piece(moment_a_ref, moment_b_ref)
    second_ref[...] = piece(second_a_ref, second_b_ref)


def adam_body(in_ref, moment_ref, second_ref, out_ref):
    step = adam_step(total_of(in_ref), moment_ref[...], second_ref[...]).astype(BF)
    for i in range(out_ref.shape[0]):
        out_ref[i] = step


def step_of_a(step_ref, rank, width):
    count, _, wide = step_ref.shape
    rows_a = rank * width // wide // count
    step = jnp.concatenate([step_ref[i].astype(F32)[:rows_a] for i in range(count)], axis=0)
    return unstack(step, rank)


def inner_body(step_ref, a_ref, flat_ref, out_ref):
    rank, width = a_ref.shape
    new_a = (a_ref[...] - learn_rate * step_of_a(step_ref, rank, width)).astype(BF)
    inner = rows_dot(new_a, flat_ref[...]).astype(BF)
    for i in range(out_ref.shape[0]):
        out_ref[i] = inner


def step_body(step_ref, b_ref, step_a_ref, step_b_ref, new_b_ref):
    count = step_ref.shape[0]
    rank, width = step_a_ref.shape
    rows_a, rows_b = rank * width // step_ref.shape[2] // count, rank // count
    step_a_ref[...] = step_of_a(step_ref, rank, width)
    parts = [step_ref[i].astype(F32)[rows_a : rows_a + rows_b] for i in range(count)]
    step_b = jnp.concatenate(parts, axis=0)
    step_b_ref[...] = step_b
    new_b_ref[...] = (b_ref[...] - learn_rate * step_b).astype(BF)


def base_body(value_ref, *refs):
    pieces, out_ref, held, value, copied = refs[:4], *refs[4:]
    core, chip = lax.axis_index("core"), lax.axis_index("zl")
    chips = value.shape[0]
    half = chips // 2
    copies = []
    for i in range(chips):
        place = lax.bitwise_xor(chip, i // half + i % half * half)
        for j in range(2):
            copies.append(
                (
                    pltpu.make_async_copy(
                        pieces[2 * j + i // half].at[i % half], held.at[i, j], copied.at[i, j, 0]
                    ),
                    pltpu.make_async_copy(
                        value_ref.at[place, core if j == 0 else 1 - core], value.at[i, j], copied.at[i, j, 1]
                    ),
                )
            )
    for pair in copies:
        for copy in pair:
            copy.start()
    total = jnp.zeros(out_ref.shape, F32)
    for i in range(chips):
        for j in range(2):
            for copy in copies[2 * i + j]:
                copy.wait()
            total += jnp.dot(held[i, j], value[i, j], preferred_element_type=F32)
    out_ref[...] = total


def cache_body(steps, q_ref, k_ref, v_ref, new_ref, length_ref, out_ref, weight_ref):
    groups, wide = length_ref.shape
    tall = q_ref.shape[0] // groups
    heads = q_ref.shape[1] // HD
    slots = wide // (tall // steps)
    row = lax.broadcasted_iota(jnp.int32, (heads * tall, wide), 0) % tall
    column = lax.broadcasted_iota(jnp.int32, (heads * tall, wide), 1)
    same = row // steps == column // slots
    slot = column % slots
    scale = 1.0 / math.sqrt(HD)
    for g in range(groups):
        query = jnp.concatenate(
            [q_ref[g * tall : (g + 1) * tall, h * HD : (h + 1) * HD] for h in range(heads)], axis=0
        )
        old = rows_dot(query, k_ref[g * wide : (g + 1) * wide, :]) * scale
        old = jnp.where(same & (slot < length_ref[g : g + 1, :]), old, -1e30)
        new = rows_dot(query, new_ref[...]) * scale
        token = column - g * tall
        seen = (token >= 0) & (token < tall) & (token // steps == row // steps) & (token <= row)
        new = jnp.where(seen, new, -1e30)
        largest = jnp.maximum(
            jnp.max(old, axis=1, keepdims=True), jnp.max(new, axis=1, keepdims=True)
        )
        old, new = jnp.exp(old - largest), jnp.exp(new - largest)
        total = jnp.sum(old, axis=1, keepdims=True) + jnp.sum(new, axis=1, keepdims=True)
        at = slice(g * heads * tall, (g + 1) * heads * tall)
        weight_ref[at, :] = (new / total).astype(BF)
        out_ref[at, :] = jnp.dot(
            (old / total).astype(BF), v_ref[g * wide : (g + 1) * wide, :], preferred_element_type=F32
        )


def last_body(groups, inner_ref, new_b_ref, base_ref, old_ref, weight_ref, out_ref):
    inner = total_of(inner_ref).astype(BF)
    change = columns_dot(inner, new_b_ref[...])
    values = (base_ref[...] + adapter_scale * change).astype(BF)
    rows, steps, wide = out_ref.shape
    each = rows // groups
    tall = each * steps
    heads = wide // HD
    for g in range(groups):
        at = slice(g * heads * tall, (g + 1) * heads * tall)
        out = old_ref[at, :] + jnp.dot(weight_ref[at, :], values, preferred_element_type=F32)
        for h in range(heads):
            part = out[h * tall : (h + 1) * tall].reshape(each, steps, HD)
            out_ref[g * each : (g + 1) * each, :, h * HD : (h + 1) * HD] = part.astype(BF)


def local(
    trainer_token_input,
    cotangent,
    adapter_a,
    adapter_b,
    moment_a,
    second_a,
    moment_b,
    second_b,
    value_matrix,
    decode_states,
    new_keys,
    queries,
    cache_keys,
    cache_values,
    lengths,
):
    pairs = lax.axis_size("zl")
    tensor = lax.axis_size(TENSOR)
    plane = lax.axis_size(PLANE)
    tokens, width = trainer_token_input.shape
    rank = adapter_a.shape[1]
    kv = cotangent.shape[1]
    rows, steps, _ = decode_states.shape
    count = rows * steps
    slots = cache_keys.shape[1]
    two = 2 * rank
    flat = lax.optimization_barrier(decode_states.reshape(count, width))
    a_turned = adapter_a.T

    half = shape((tokens // 2, two), F32)
    starts = (trainer_token_input, cotangent, a_turned, adapter_b)
    mine, theirs = call(low_body, (half, half), *map(far, starts))
    pair = call(pair_body, shape((pairs, tokens // 2, two), BF), mine, swap(theirs))

    pair, send = lax.optimization_barrier((pair, flat))
    second_chip = reach(send[None], 2)
    mine = jnp.sum(trade(pair, "zl").astype(F32), axis=0).astype(BF)
    theirs = swap(mine)

    rows_a, rows_b = rank * width // kv // plane, rank // plane
    deep = rows_a + rows_b + -(rows_a + rows_b) % 16
    scale = adapter_scale / (tokens * lax.axis_size(DP))
    block = call(
        lambda *refs: gradient_body(scale, *refs),
        shape((plane, deep, kv), BF),
        trainer_token_input,
        cotangent,
        mine,
        theirs,
    )

    shard = trade(block, PLANE)
    near = jnp.concatenate([send[None], second_chip], axis=0)
    distant = reach(near, 1)
    shard = call(sum_body, shape((lax.axis_size("zh"), deep, kv), F32), shard)
    shard, moments = lax.optimization_barrier(
        (shard, (moment_a.T, second_a.T, moment_b, second_b))
    )
    shard = trade(shard, "zh")
    piece = shape((deep, kv), F32)
    moments = call(shard_body, (piece, piece), *map(far, moments))
    near_other = swap(near)
    step = call(adam_body, shape((plane, deep, kv), BF), shard, *moments)
    step, query = lax.optimization_barrier((step, queries))
    step = trade(step, PLANE)
    groups = rows * slots // HD
    heads = queries.shape[2] // HD
    old, weights = call(
        lambda *refs: cache_body(steps, *refs),
        (shape((count * heads, HD), F32), shape((count * heads, count), BF)),
        query.reshape(count, heads * HD),
        far(cache_keys.reshape(rows * slots, kv)),
        far(cache_values.reshape(rows * slots, kv)),
        new_keys.reshape(count, kv),
        jnp.repeat(lengths, slots).reshape(groups, HD),
        flops=2 * count * heads * HD * HD * 3,
        moved=8 * 2**20,
    )
    step, old, weights = lax.optimization_barrier((step, old, weights))
    distant_other = swap(distant)

    inner = call(inner_body, shape((tensor, rank, count), BF), step, a_turned, flat)
    inner = trade(inner, TENSOR)
    step_a, step_b, new_b = call(
        step_body, (shape((rank, width), F32), shape((rank, kv), F32), shape((rank, kv), BF)), step, adapter_b
    )
    base = call(
        base_body,
        shape((count, kv), F32),
        *map(far, (value_matrix.reshape(pairs, 2, width, kv), near, distant, near_other, distant_other)),
        flops=2 * count * tensor * width * kv,
        moved=4 * 2**20,
        in_specs=[pl.BlockSpec(memory_space=pl.ANY)] * 5,
        scratch_shapes=[
            pltpu.VMEM((pairs, 2, count, width), BF),
            pltpu.VMEM((pairs, 2, width, kv), BF),
            pltpu.SemaphoreType.DMA((pairs, 2, 2)),
        ],
    )

    attended = call(
        lambda *refs: last_body(groups, *refs),
        shape((rows, steps, heads * HD), BF),
        inner,
        new_b,
        base,
        old,
        weights,
    )
    return (step_a.T, step_b, attended)


def solution(mesh):
    sizes = (4, 4, 4, mesh.devices.shape[1] // 2, 2)
    fine = Mesh(mesh.devices.reshape(sizes), DP + TENSOR)
    return jax.shard_map(
        local,
        mesh=fine,
        in_specs=(
            P(DP, TENSOR),
            P(DP, TENSOR),
            P(TENSOR, None),
            P(None, TENSOR),
            P(TENSOR, None),
            P(TENSOR, None),
            P(None, TENSOR),
            P(None, TENSOR),
            P(None, TENSOR),
            P(DP, None, TENSOR),
            P(DP, None, TENSOR),
            P(DP, None, TENSOR),
            P(DP, None, TENSOR),
            P(DP, None, TENSOR),
            P(DP),
        ),
        out_specs=(P(TENSOR, None), P(None, TENSOR), P(DP, None, TENSOR)),
        check_vma=False,
    )
```

```python
import math

import jax
import jax.numpy as jnp
from jax import lax
from jax.experimental import pallas as pl
from jax.experimental.pallas import tpu as pltpu
from jax.sharding import Mesh, PartitionSpec as P

HD = 128


adapter_scale = 2.0
learn_rate = 0.001
beta_one = 0.9
beta_two = 0.999
adam_eps = 1e-08
first_fix = 1.0 - 0.9**10
second_fix = 1.0 - 0.999**10

DP = ("x", "zh", "y")
PLANE = ("x", "y")
TENSOR = ("zl", "core")
BF = jnp.bfloat16
F32 = jnp.float32


def adam_step(grad, moment, second):
    moment_new = beta_one * moment + (1.0 - beta_one) * grad
    second_new = beta_two * second + (1.0 - beta_two) * grad * grad
    return moment_new / first_fix / (jnp.sqrt(second_new / second_fix) + adam_eps)


def trade(parts, axes):
    return lax.all_to_all(parts, axes, 0, 0, tiled=True)


def swap(value):
    return lax.ppermute(value, "core", [(0, 1), (1, 0)])


def reach(value, hop):
    return lax.ppermute(value, "zl", [(i, i ^ hop) for i in range(lax.axis_size("zl"))])


def call(body, out, *args, flops=0, moved=0, **more):
    return pl.pallas_call(
        body,
        out_shape=out,
        cost_estimate=pl.CostEstimate(flops=flops, bytes_accessed=moved, transcendentals=0),
        compiler_params=pltpu.CompilerParams(vmem_limit_bytes=16 * 2**20),
        **more,
    )(*args)


def far(value):
    return pltpu.with_memory_space_constraint(value, pltpu.HBM)


def shape(dims, kind):
    return jax.ShapeDtypeStruct(dims, kind)


def columns_dot(a, b):
    return lax.dot_general(a, b, (((0,), (0,)), ((), ())), preferred_element_type=F32)


def rows_dot(a, b):
    return lax.dot_general(a, b, (((1,), (1,)), ((), ())), preferred_element_type=F32)


def low_body(x_ref, cot_ref, a_ref, b_ref, mine_ref, theirs_ref):
    acts = rows_dot(x_ref[...], a_ref[...].astype(BF))
    grads = rows_dot(cot_ref[...], b_ref[...].astype(BF))
    both = jnp.concatenate([acts, grads], axis=1)
    half = both.shape[0] // 2
    first = lax.axis_index("core") == 0
    mine_ref[...] = jnp.where(first, both[:half], both[half:])
    theirs_ref[...] = jnp.where(first, both[half:], both[:half])


def pair_body(mine_ref, theirs_ref, out_ref):
    total = (mine_ref[...] + theirs_ref[...]).astype(BF)
    for i in range(out_ref.shape[0]):
        out_ref[i] = total


def stack(value, wide):
    return jnp.concatenate([value[:, i : i + wide] for i in range(0, value.shape[1], wide)], axis=0)


def unstack(value, tall):
    return jnp.concatenate([value[i : i + tall] for i in range(0, value.shape[0], tall)], axis=1)


def gradient_body(scale, x_ref, cot_ref, mine_ref, theirs_ref, out_ref):
    mine, theirs = mine_ref[...].astype(F32), theirs_ref[...].astype(F32)
    first = lax.axis_index("core") == 0
    low = jnp.concatenate([jnp.where(first, mine, theirs), jnp.where(first, theirs, mine)], axis=0)
    rank = low.shape[1] // 2
    low = low.astype(BF)
    count, deep, wide = out_ref.shape
    grad_a = stack(columns_dot(low, x_ref[...])[rank:], wide) * scale
    grad_b = columns_dot(low, cot_ref[...])[:rank] * scale
    rows_a, rows_b = grad_a.shape[0] // count, rank // count
    blank = jnp.zeros((deep - rows_a - rows_b, wide), F32)
    for i in range(count):
        parts = [grad_a[i * rows_a : (i + 1) * rows_a], grad_b[i * rows_b : (i + 1) * rows_b], blank]
        out_ref[i] = jnp.concatenate(parts, axis=0).astype(BF)


def total_of(ref):
    total = ref[0].astype(F32)
    for i in range(1, ref.shape[0]):
        total = total + ref[i].astype(F32)
    return total


def sum_body(in_ref, out_ref):
    total = total_of(in_ref)
    for i in range(out_ref.shape[0]):
        out_ref[i] = total


def shard_body(moment_a_ref, second_a_ref, moment_b_ref, second_b_ref, moment_ref, second_ref):
    deep, wide = moment_ref.shape
    rank = moment_a_ref.shape[0]
    count = lax.axis_size(PLANE)
    rows_a, rows_b = rank * moment_a_ref.shape[1] // wide // count, rank // count
    place = lax.axis_index(PLANE)
    column = pl.multiple_of(place * rows_a // rank * wide, wide)
    row = pl.multiple_of(lax.rem(place * rows_a, rank), rows_a)
    most = max(rows_b, 8)
    row_b = pl.multiple_of(place * rows_b // most * most, most)

    def piece(a_ref, b_ref):
        of_b = b_ref[pl.ds(row_b, most), :]
        chosen = of_b[:rows_b]
        for i in range(rows_b, most, rows_b):
            chosen = jnp.where(place * rows_b == row_b + i, of_b[i : i + rows_b], chosen)
        pad = jnp.ones((deep - rows_a - rows_b, wide), F32)
        return jnp.concatenate([a_ref[pl.ds(row, rows_a), pl.ds(column, wide)], chosen, pad], axis=0)

    moment_ref[...] = piece(moment_a_ref, moment_b_ref)
    second_ref[...] = piece(second_a_ref, second_b_ref)


def adam_body(in_ref, moment_ref, second_ref, out_ref):
    step = adam_step(total_of(in_ref), moment_ref[...], second_ref[...]).astype(BF)
    for i in range(out_ref.shape[0]):
        out_ref[i] = step


def step_of_a(step_ref, rank, width):
    count, _, wide = step_ref.shape
    rows_a = rank * width // wide // count
    step = jnp.concatenate([step_ref[i].astype(F32)[:rows_a] for i in range(count)], axis=0)
    return unstack(step, rank)


def inner_body(step_ref, a_ref, flat_ref, out_ref):
    rank, width = a_ref.shape
    new_a = (a_ref[...] - learn_rate * step_of_a(step_ref, rank, width)).astype(BF)
    inner = rows_dot(new_a, flat_ref[...]).astype(BF)
    for i in range(out_ref.shape[0]):
        out_ref[i] = inner


def step_body(step_ref, b_ref, step_a_ref, step_b_ref, new_b_ref):
    count = step_ref.shape[0]
    rank, width = step_a_ref.shape
    rows_a, rows_b = rank * width // step_ref.shape[2] // count, rank // count
    step_a_ref[...] = step_of_a(step_ref, rank, width)
    parts = [step_ref[i].astype(F32)[rows_a : rows_a + rows_b] for i in range(count)]
    step_b = jnp.concatenate(parts, axis=0)
    step_b_ref[...] = step_b
    new_b_ref[...] = (b_ref[...] - learn_rate * step_b).astype(BF)


def base_body(value_ref, *refs):
    pieces, out_ref, held, value, copied = refs[:4], *refs[4:]
    core, chip = lax.axis_index("core"), lax.axis_index("zl")
    chips = value.shape[0]
    half = chips // 2
    copies = []
    for i in range(chips):
        place = lax.bitwise_xor(chip, i // half + i % half * half)
        for j in range(2):
            copies.append(
                (
                    pltpu.make_async_copy(
                        pieces[2 * j + i // half].at[i % half], held.at[i, j], copied.at[i, j, 0]
                    ),
                    pltpu.make_async_copy(
                        value_ref.at[place, core if j == 0 else 1 - core], value.at[i, j], copied.at[i, j, 1]
                    ),
                )
            )
    for pair in copies:
        for copy in pair:
            copy.start()
    total = jnp.zeros(out_ref.shape, F32)
    for i in range(chips):
        for j in range(2):
            for copy in copies[2 * i + j]:
                copy.wait()
            total += jnp.dot(held[i, j], value[i, j], preferred_element_type=F32)
    out_ref[...] = total


def cache_body(steps, q_ref, k_ref, v_ref, new_ref, length_ref, out_ref, weight_ref):
    groups, wide = length_ref.shape
    tall = q_ref.shape[0] // groups
    heads = q_ref.shape[1] // HD
    slots = wide // (tall // steps)
    row = lax.broadcasted_iota(jnp.int32, (heads * tall, wide), 0) % tall
    column = lax.broadcasted_iota(jnp.int32, (heads * tall, wide), 1)
    same = row // steps == column // slots
    slot = column % slots
    scale = 1.0 / math.sqrt(HD)
    for g in range(groups):
        query = jnp.concatenate(
            [q_ref[g * tall : (g + 1) * tall, h * HD : (h + 1) * HD] for h in range(heads)], axis=0
        )
        old = rows_dot(query, k_ref[g * wide : (g + 1) * wide, :]) * scale
        old = jnp.where(same & (slot < length_ref[g : g + 1, :]), old, -1e30)
        new = rows_dot(query, new_ref[...]) * scale
        token = column - g * tall
        seen = (token >= 0) & (token < tall) & (token // steps == row // steps) & (token <= row)
        new = jnp.where(seen, new, -1e30)
        largest = jnp.maximum(
            jnp.max(old, axis=1, keepdims=True), jnp.max(new, axis=1, keepdims=True)
        )
        old, new = jnp.exp(old - largest), jnp.exp(new - largest)
        total = jnp.sum(old, axis=1, keepdims=True) + jnp.sum(new, axis=1, keepdims=True)
        at = slice(g * heads * tall, (g + 1) * heads * tall)
        weight_ref[at, :] = (new / total).astype(BF)
        out_ref[at, :] = jnp.dot(
            (old / total).astype(BF), v_ref[g * wide : (g + 1) * wide, :], preferred_element_type=F32
        )


def last_body(groups, inner_ref, new_b_ref, base_ref, old_ref, weight_ref, out_ref):
    inner = total_of(inner_ref).astype(BF)
    change = columns_dot(inner, new_b_ref[...])
    values = (base_ref[...] + adapter_scale * change).astype(BF)
    rows, steps, wide = out_ref.shape
    each = rows // groups
    tall = each * steps
    heads = wide // HD
    for g in range(groups):
        at = slice(g * heads * tall, (g + 1) * heads * tall)
        out = old_ref[at, :] + jnp.dot(weight_ref[at, :], values, preferred_element_type=F32)
        for h in range(heads):
            part = out[h * tall : (h + 1) * tall].reshape(each, steps, HD)
            out_ref[g * each : (g + 1) * each, :, h * HD : (h + 1) * HD] = part.astype(BF)


def local(
    trainer_token_input,
    cotangent,
    adapter_a,
    adapter_b,
    moment_a,
    second_a,
    moment_b,
    second_b,
    value_matrix,
    decode_states,
    new_keys,
    queries,
    cache_keys,
    cache_values,
    lengths,
):
    pairs = lax.axis_size("zl")
    tensor = lax.axis_size(TENSOR)
    plane = lax.axis_size(PLANE)
    tokens, width = trainer_token_input.shape
    rank = adapter_a.shape[1]
    kv = cotangent.shape[1]
    rows, steps, _ = decode_states.shape
    count = rows * steps
    slots = cache_keys.shape[1]
    two = 2 * rank
    flat = lax.optimization_barrier(decode_states.reshape(count, width))
    a_turned = adapter_a.T

    half = shape((tokens // 2, two), F32)
    starts = (trainer_token_input, cotangent, a_turned, adapter_b)
    mine, theirs = call(low_body, (half, half), *map(far, starts))
    pair = call(pair_body, shape((pairs, tokens // 2, two), BF), mine, swap(theirs))

    pair, send = lax.optimization_barrier((pair, flat))
    second_chip = reach(send[None], 2)
    mine = jnp.sum(trade(pair, "zl").astype(F32), axis=0).astype(BF)
    theirs = swap(mine)

    rows_a, rows_b = rank * width // kv // plane, rank // plane
    deep = rows_a + rows_b + -(rows_a + rows_b) % 16
    scale = adapter_scale / (tokens * lax.axis_size(DP))
    block = call(
        lambda *refs: gradient_body(scale, *refs),
        shape((plane, deep, kv), BF),
        trainer_token_input,
        cotangent,
        mine,
        theirs,
    )

    shard = trade(block, PLANE)
    near = jnp.concatenate([send[None], second_chip], axis=0)
    distant = reach(near, 1)
    shard = call(sum_body, shape((lax.axis_size("zh"), deep, kv), F32), shard)
    shard, query, moments = lax.optimization_barrier(
        (shard, queries, (moment_a.T, second_a.T, moment_b, second_b))
    )
    shard = trade(shard, "zh")
    piece = shape((deep, kv), F32)
    moments = call(shard_body, (piece, piece), *map(far, moments))

    groups = rows * slots // HD
    heads = queries.shape[2] // HD
    old, weights = call(
        lambda *refs: cache_body(steps, *refs),
        (shape((count * heads, HD), F32), shape((count * heads, count), BF)),
        query.reshape(count, heads * HD),
        cache_keys.reshape(rows * slots, kv),
        cache_values.reshape(rows * slots, kv),
        new_keys.reshape(count, kv),
        jnp.repeat(lengths, slots).reshape(groups, HD),
        flops=2 * count * heads * HD * HD * 3,
        moved=8 * 2**20,
    )
    shard, old, weights = lax.optimization_barrier((shard, old, weights))
    step = call(adam_body, shape((plane, deep, kv), BF), shard, *moments)
    distant_sent, near_sent, _ = lax.optimization_barrier((distant, near, step))
    distant_other, near_other = swap(distant_sent), swap(near_sent)
    step = trade(step, PLANE)

    inner = call(inner_body, shape((tensor, rank, count), BF), step, a_turned, flat)
    inner = trade(inner, TENSOR)
    step_a, step_b, new_b = call(
        step_body, (shape((rank, width), F32), shape((rank, kv), F32), shape((rank, kv), BF)), step, adapter_b
    )
    base = call(
        base_body,
        shape((count, kv), F32),
        *map(far, (value_matrix.reshape(pairs, 2, width, kv), near, distant, near_other, distant_other)),
        flops=2 * count * tensor * width * kv,
        moved=4 * 2**20,
        in_specs=[pl.BlockSpec(memory_space=pl.ANY)] * 5,
        scratch_shapes=[
            pltpu.VMEM((pairs, 2, count, width), BF),
            pltpu.VMEM((pairs, 2, width, kv), BF),
            pltpu.SemaphoreType.DMA((pairs, 2, 2)),
        ],
    )

    attended = call(
        lambda *refs: last_body(groups, *refs),
        shape((rows, steps, heads * HD), BF),
        inner,
        new_b,
        base,
        old,
        weights,
    )
    return (step_a.T, step_b, attended)


def solution(mesh):
    sizes = (4, 4, 4, mesh.devices.shape[1] // 2, 2)
    fine = Mesh(mesh.devices.reshape(sizes), DP + TENSOR)
    return jax.shard_map(
        local,
        mesh=fine,
        in_specs=(
            P(DP, TENSOR),
            P(DP, TENSOR),
            P(TENSOR, None),
            P(None, TENSOR),
            P(TENSOR, None),
            P(TENSOR, None),
            P(None, TENSOR),
            P(None, TENSOR),
            P(None, TENSOR),
            P(DP, None, TENSOR),
            P(DP, None, TENSOR),
            P(DP, None, TENSOR),
            P(DP, None, TENSOR),
            P(DP, None, TENSOR),
            P(DP),
        ),
        out_specs=(P(TENSOR, None), P(None, TENSOR), P(DP, None, TENSOR)),
        check_vma=False,
    )
```

```python
import math

import jax
import jax.numpy as jnp
from jax import lax
from jax.experimental import pallas as pl
from jax.experimental.pallas import tpu as pltpu
from jax.sharding import Mesh, PartitionSpec as P

HD = 128


adapter_scale = 2.0
learn_rate = 0.001
beta_one = 0.9
beta_two = 0.999
adam_eps = 1e-08
first_fix = 1.0 - 0.9**10
second_fix = 1.0 - 0.999**10

DP = ("x", "zh", "y")
PLANE = ("x", "y")
TENSOR = ("zl", "core")
BF = jnp.bfloat16
F32 = jnp.float32


def adam_step(grad, moment, second):
    moment_new = beta_one * moment + (1.0 - beta_one) * grad
    second_new = beta_two * second + (1.0 - beta_two) * grad * grad
    return moment_new / first_fix / (jnp.sqrt(second_new / second_fix) + adam_eps)


def trade(parts, axes):
    return lax.all_to_all(parts, axes, 0, 0, tiled=True)


def swap(value):
    return lax.ppermute(value, "core", [(0, 1), (1, 0)])


def reach(value, hop):
    return lax.ppermute(value, "zl", [(i, i ^ hop) for i in range(lax.axis_size("zl"))])


def call(body, out, *args, flops=0, moved=0, **more):
    return pl.pallas_call(
        body,
        out_shape=out,
        cost_estimate=pl.CostEstimate(flops=flops, bytes_accessed=moved, transcendentals=0),
        compiler_params=pltpu.CompilerParams(vmem_limit_bytes=16 * 2**20),
        **more,
    )(*args)


def far(value):
    return pltpu.with_memory_space_constraint(value, pltpu.HBM)


def shape(dims, kind):
    return jax.ShapeDtypeStruct(dims, kind)


def columns_dot(a, b):
    return lax.dot_general(a, b, (((0,), (0,)), ((), ())), preferred_element_type=F32)


def rows_dot(a, b):
    return lax.dot_general(a, b, (((1,), (1,)), ((), ())), preferred_element_type=F32)


def low_body(x_ref, cot_ref, a_ref, b_ref, out_ref):
    acts = rows_dot(x_ref[...], a_ref[...].astype(BF))
    grads = rows_dot(cot_ref[...], b_ref[...].astype(BF))
    both = jnp.concatenate([acts, grads], axis=1).astype(BF)
    tall = out_ref.shape[1]
    for i in range(out_ref.shape[0]):
        core = i % 2
        out_ref[i] = both[core * tall : (core + 1) * tall]


def stack(value, wide):
    return jnp.concatenate([value[:, i : i + wide] for i in range(0, value.shape[1], wide)], axis=0)


def unstack(value, tall):
    return jnp.concatenate([value[i : i + tall] for i in range(0, value.shape[0], tall)], axis=1)


def gradient_body(scale, x_ref, cot_ref, mine_ref, theirs_ref, out_ref):
    mine, theirs = mine_ref[...].astype(F32), theirs_ref[...].astype(F32)
    first = lax.axis_index("core") == 0
    low = jnp.concatenate([jnp.where(first, mine, theirs), jnp.where(first, theirs, mine)], axis=0)
    rank = low.shape[1] // 2
    low = low.astype(BF)
    count, deep, wide = out_ref.shape
    grad_a = stack(columns_dot(low, x_ref[...])[rank:], wide) * scale
    grad_b = columns_dot(low, cot_ref[...])[:rank] * scale
    rows_a, rows_b = grad_a.shape[0] // count, rank // count
    blank = jnp.zeros((deep - rows_a - rows_b, wide), F32)
    for i in range(count):
        parts = [grad_a[i * rows_a : (i + 1) * rows_a], grad_b[i * rows_b : (i + 1) * rows_b], blank]
        out_ref[i] = jnp.concatenate(parts, axis=0).astype(BF)


def total_of(ref):
    total = ref[0].astype(F32)
    for i in range(1, ref.shape[0]):
        total = total + ref[i].astype(F32)
    return total


def sum_body(in_ref, out_ref):
    total = total_of(in_ref)
    for i in range(out_ref.shape[0]):
        out_ref[i] = total


def shard_body(moment_a_ref, second_a_ref, moment_b_ref, second_b_ref, moment_ref, second_ref):
    deep, wide = moment_ref.shape
    rank = moment_a_ref.shape[0]
    count = lax.axis_size(PLANE)
    rows_a, rows_b = rank * moment_a_ref.shape[1] // wide // count, rank // count
    place = lax.axis_index(PLANE)
    column = pl.multiple_of(place * rows_a // rank * wide, wide)
    row = pl.multiple_of(lax.rem(place * rows_a, rank), rows_a)
    most = max(rows_b, 8)
    row_b = pl.multiple_of(place * rows_b // most * most, most)

    def piece(a_ref, b_ref):
        of_b = b_ref[pl.ds(row_b, most), :]
        chosen = of_b[:rows_b]
        for i in range(rows_b, most, rows_b):
            chosen = jnp.where(place * rows_b == row_b + i, of_b[i : i + rows_b], chosen)
        pad = jnp.ones((deep - rows_a - rows_b, wide), F32)
        return jnp.concatenate([a_ref[pl.ds(row, rows_a), pl.ds(column, wide)], chosen, pad], axis=0)

    moment_ref[...] = piece(moment_a_ref, moment_b_ref)
    second_ref[...] = piece(second_a_ref, second_b_ref)


def adam_body(in_ref, moment_ref, second_ref, out_ref):
    step = adam_step(total_of(in_ref), moment_ref[...], second_ref[...]).astype(BF)
    for i in range(out_ref.shape[0]):
        out_ref[i] = step


def step_of_a(step_ref, rank, width):
    count, _, wide = step_ref.shape
    rows_a = rank * width // wide // count
    step = jnp.concatenate([step_ref[i].astype(F32)[:rows_a] for i in range(count)], axis=0)
    return unstack(step, rank)


def inner_body(step_ref, a_ref, flat_ref, out_ref):
    rank, width = a_ref.shape
    new_a = (a_ref[...] - learn_rate * step_of_a(step_ref, rank, width)).astype(BF)
    inner = rows_dot(new_a, flat_ref[...]).astype(BF)
    for i in range(out_ref.shape[0]):
        out_ref[i] = inner


def step_body(step_ref, b_ref, step_a_ref, step_b_ref, new_b_ref):
    count = step_ref.shape[0]
    rank, width = step_a_ref.shape
    rows_a, rows_b = rank * width // step_ref.shape[2] // count, rank // count
    step_a_ref[...] = step_of_a(step_ref, rank, width)
    parts = [step_ref[i].astype(F32)[rows_a : rows_a + rows_b] for i in range(count)]
    step_b = jnp.concatenate(parts, axis=0)
    step_b_ref[...] = step_b
    new_b_ref[...] = (b_ref[...] - learn_rate * step_b).astype(BF)


def base_body(value_ref, *refs):
    pieces, out_ref, held, value, copied = refs[:4], *refs[4:]
    core, chip = lax.axis_index("core"), lax.axis_index("zl")
    chips = value.shape[0]
    half = chips // 2
    copies = []
    for i in range(chips):
        place = lax.bitwise_xor(chip, i // half + i % half * half)
        for j in range(2):
            copies.append(
                (
                    pltpu.make_async_copy(
                        pieces[2 * j + i // half].at[i % half], held.at[i, j], copied.at[i, j, 0]
                    ),
                    pltpu.make_async_copy(
                        value_ref.at[place, core if j == 0 else 1 - core], value.at[i, j], copied.at[i, j, 1]
                    ),
                )
            )
    for pair in copies:
        for copy in pair:
            copy.start()
    total = jnp.zeros(out_ref.shape, F32)
    for i in range(chips):
        for j in range(2):
            for copy in copies[2 * i + j]:
                copy.wait()
            total += jnp.dot(held[i, j], value[i, j], preferred_element_type=F32)
    out_ref[...] = total


def cache_body(steps, q_ref, k_ref, v_ref, new_ref, length_ref, out_ref, weight_ref):
    groups, wide = length_ref.shape
    tall = q_ref.shape[0] // groups
    heads = q_ref.shape[1] // HD
    slots = wide // (tall // steps)
    row = lax.broadcasted_iota(jnp.int32, (heads * tall, wide), 0) % tall
    column = lax.broadcasted_iota(jnp.int32, (heads * tall, wide), 1)
    same = row // steps == column // slots
    slot = column % slots
    scale = 1.0 / math.sqrt(HD)
    for g in range(groups):
        query = jnp.concatenate(
            [q_ref[g * tall : (g + 1) * tall, h * HD : (h + 1) * HD] for h in range(heads)], axis=0
        )
        old = rows_dot(query, k_ref[g * wide : (g + 1) * wide, :]) * scale
        old = jnp.where(same & (slot < length_ref[g : g + 1, :]), old, -1e30)
        new = rows_dot(query, new_ref[...]) * scale
        token = column - g * tall
        seen = (token >= 0) & (token < tall) & (token // steps == row // steps) & (token <= row)
        new = jnp.where(seen, new, -1e30)
        largest = jnp.maximum(
            jnp.max(old, axis=1, keepdims=True), jnp.max(new, axis=1, keepdims=True)
        )
        old, new = jnp.exp(old - largest), jnp.exp(new - largest)
        total = jnp.sum(old, axis=1, keepdims=True) + jnp.sum(new, axis=1, keepdims=True)
        at = slice(g * heads * tall, (g + 1) * heads * tall)
        weight_ref[at, :] = (new / total).astype(BF)
        out_ref[at, :] = jnp.dot(
            (old / total).astype(BF), v_ref[g * wide : (g + 1) * wide, :], preferred_element_type=F32
        )


def last_body(groups, inner_ref, new_b_ref, base_ref, old_ref, weight_ref, out_ref):
    inner = total_of(inner_ref).astype(BF)
    change = columns_dot(inner, new_b_ref[...])
    values = (base_ref[...] + adapter_scale * change).astype(BF)
    rows, steps, wide = out_ref.shape
    each = rows // groups
    tall = each * steps
    heads = wide // HD
    for g in range(groups):
        at = slice(g * heads * tall, (g + 1) * heads * tall)
        out = old_ref[at, :] + jnp.dot(weight_ref[at, :], values, preferred_element_type=F32)
        for h in range(heads):
            part = out[h * tall : (h + 1) * tall].reshape(each, steps, HD)
            out_ref[g * each : (g + 1) * each, :, h * HD : (h + 1) * HD] = part.astype(BF)


def local(
    trainer_token_input,
    cotangent,
    adapter_a,
    adapter_b,
    moment_a,
    second_a,
    moment_b,
    second_b,
    value_matrix,
    decode_states,
    new_keys,
    queries,
    cache_keys,
    cache_values,
    lengths,
):
    pairs = lax.axis_size("zl")
    tensor = lax.axis_size(TENSOR)
    plane = lax.axis_size(PLANE)
    tokens, width = trainer_token_input.shape
    rank = adapter_a.shape[1]
    kv = cotangent.shape[1]
    rows, steps, _ = decode_states.shape
    count = rows * steps
    slots = cache_keys.shape[1]
    two = 2 * rank
    flat = lax.optimization_barrier(decode_states.reshape(count, width))
    a_turned = adapter_a.T

    starts = (trainer_token_input, cotangent, a_turned, adapter_b)
    parts = call(low_body, shape((tensor, tokens // 2, two), BF), *map(far, starts))

    send, _ = lax.optimization_barrier((flat, parts))
    second_chip = reach(send[None], 2)
    mine = jnp.sum(trade(parts, TENSOR).astype(F32), axis=0).astype(BF)
    mine, moments = lax.optimization_barrier((mine, (moment_a.T, second_a.T, moment_b, second_b)))
    theirs = swap(mine)
    rows_a, rows_b = rank * width // kv // plane, rank // plane
    deep = rows_a + rows_b + -(rows_a + rows_b) % 16
    piece = shape((deep, kv), F32)
    moments = call(shard_body, (piece, piece), *map(far, moments))
    theirs, moments = lax.optimization_barrier((theirs, moments))

    scale = adapter_scale / (tokens * lax.axis_size(DP))
    block = call(
        lambda *refs: gradient_body(scale, *refs),
        shape((plane, deep, kv), BF),
        trainer_token_input,
        cotangent,
        mine,
        theirs,
    )

    shard = trade(block, PLANE)
    near = jnp.concatenate([send[None], second_chip], axis=0)
    distant = reach(near, 1)
    shard = call(sum_body, shape((lax.axis_size("zh"), deep, kv), F32), shard)
    shard, query = lax.optimization_barrier((shard, queries))
    shard = trade(shard, "zh")

    groups = rows * slots // HD
    heads = queries.shape[2] // HD
    old, weights = call(
        lambda *refs: cache_body(steps, *refs),
        (shape((count * heads, HD), F32), shape((count * heads, count), BF)),
        query.reshape(count, heads * HD),
        cache_keys.reshape(rows * slots, kv),
        cache_values.reshape(rows * slots, kv),
        new_keys.reshape(count, kv),
        jnp.repeat(lengths, slots).reshape(groups, HD),
        flops=2 * count * heads * HD * HD * 3,
        moved=8 * 2**20,
    )
    shard, old, weights = lax.optimization_barrier((shard, old, weights))
    step = call(adam_body, shape((plane, deep, kv), BF), shard, *moments)
    distant_sent, near_sent, _ = lax.optimization_barrier((distant, near, step))
    distant_other, near_other = swap(distant_sent), swap(near_sent)
    step = trade(step, PLANE)

    inner = call(inner_body, shape((tensor, rank, count), BF), step, a_turned, flat)
    inner = trade(inner, TENSOR)
    step_a, step_b, new_b = call(
        step_body, (shape((rank, width), F32), shape((rank, kv), F32), shape((rank, kv), BF)), step, adapter_b
    )
    base = call(
        base_body,
        shape((count, kv), F32),
        far(value_matrix.reshape(pairs, 2, width, kv)),
        near,
        distant,
        near_other,
        distant_other,
        flops=2 * count * tensor * width * kv,
        moved=4 * 2**20,
        in_specs=[pl.BlockSpec(memory_space=pl.ANY)] * 5,
        scratch_shapes=[
            pltpu.VMEM((pairs, 2, count, width), BF),
            pltpu.VMEM((pairs, 2, width, kv), BF),
            pltpu.SemaphoreType.DMA((pairs, 2, 2)),
        ],
    )

    attended = call(
        lambda *refs: last_body(groups, *refs),
        shape((rows, steps, heads * HD), BF),
        inner,
        new_b,
        base,
        old,
        weights,
    )
    return (step_a.T, step_b, attended)


def solution(mesh):
    sizes = (4, 4, 4, mesh.devices.shape[1] // 2, 2)
    fine = Mesh(mesh.devices.reshape(sizes), DP + TENSOR)
    return jax.shard_map(
        local,
        mesh=fine,
        in_specs=(
            P(DP, TENSOR),
            P(DP, TENSOR),
            P(TENSOR, None),
            P(None, TENSOR),
            P(TENSOR, None),
            P(TENSOR, None),
            P(None, TENSOR),
            P(None, TENSOR),
            P(None, TENSOR),
            P(DP, None, TENSOR),
            P(DP, None, TENSOR),
            P(DP, None, TENSOR),
            P(DP, None, TENSOR),
            P(DP, None, TENSOR),
            P(DP),
        ),
        out_specs=(P(TENSOR, None), P(None, TENSOR), P(DP, None, TENSOR)),
        check_vma=False,
    )
```

```python
import math

import jax
import jax.numpy as jnp
from jax import lax
from jax.experimental import pallas as pl
from jax.experimental.pallas import tpu as pltpu
from jax.sharding import Mesh, PartitionSpec as P

HD = 128


adapter_scale = 2.0
learn_rate = 0.001
beta_one = 0.9
beta_two = 0.999
adam_eps = 1e-08
first_fix = 1.0 - 0.9**10
second_fix = 1.0 - 0.999**10

DP = ("x", "zh", "y")
PLANE = ("x", "y")
TENSOR = ("zl", "core")
BF = jnp.bfloat16
F32 = jnp.float32


def adam_step(grad, moment, second):
    moment_new = beta_one * moment + (1.0 - beta_one) * grad
    second_new = beta_two * second + (1.0 - beta_two) * grad * grad
    return moment_new / first_fix / (jnp.sqrt(second_new / second_fix) + adam_eps)


def trade(parts, axes):
    return lax.all_to_all(parts, axes, 0, 0, tiled=True)


def swap(value):
    return lax.ppermute(value, "core", [(0, 1), (1, 0)])


def reach(value, hop):
    return lax.ppermute(value, "zl", [(i, i ^ hop) for i in range(lax.axis_size("zl"))])


def call(body, out, *args, flops=0, moved=0, **more):
    return pl.pallas_call(
        body,
        out_shape=out,
        cost_estimate=pl.CostEstimate(flops=flops, bytes_accessed=moved, transcendentals=0),
        compiler_params=pltpu.CompilerParams(vmem_limit_bytes=16 * 2**20),
        **more,
    )(*args)


def far(value):
    return pltpu.with_memory_space_constraint(value, pltpu.HBM)


def shape(dims, kind):
    return jax.ShapeDtypeStruct(dims, kind)


def columns_dot(a, b):
    return lax.dot_general(a, b, (((0,), (0,)), ((), ())), preferred_element_type=F32)


def rows_dot(a, b):
    return lax.dot_general(a, b, (((1,), (1,)), ((), ())), preferred_element_type=F32)


def low_body(x_ref, cot_ref, a_ref, b_ref, mine_ref, theirs_ref):
    acts = rows_dot(x_ref[...], a_ref[...].astype(BF))
    grads = rows_dot(cot_ref[...], b_ref[...].astype(BF))
    both = jnp.concatenate([acts, grads], axis=1)
    half = both.shape[0] // 2
    first = lax.axis_index("core") == 0
    mine_ref[...] = jnp.where(first, both[:half], both[half:])
    theirs_ref[...] = jnp.where(first, both[half:], both[:half])


def pair_body(mine_ref, theirs_ref, out_ref):
    total = (mine_ref[...] + theirs_ref[...]).astype(BF)
    for i in range(out_ref.shape[0]):
        out_ref[i] = total


def stack(value, wide):
    return jnp.concatenate([value[:, i : i + wide] for i in range(0, value.shape[1], wide)], axis=0)


def unstack(value, tall):
    return jnp.concatenate([value[i : i + tall] for i in range(0, value.shape[0], tall)], axis=1)


def gradient_body(scale, x_ref, cot_ref, mine_ref, theirs_ref, out_ref):
    mine, theirs = mine_ref[...].astype(F32), theirs_ref[...].astype(F32)
    first = lax.axis_index("core") == 0
    low = jnp.concatenate([jnp.where(first, mine, theirs), jnp.where(first, theirs, mine)], axis=0)
    rank = low.shape[1] // 2
    low = low.astype(BF)
    count, deep, wide = out_ref.shape
    grad_a = stack(columns_dot(low, x_ref[...])[rank:], wide) * scale
    grad_b = columns_dot(low, cot_ref[...])[:rank] * scale
    rows_a, rows_b = grad_a.shape[0] // count, rank // count
    blank = jnp.zeros((deep - rows_a - rows_b, wide), F32)
    for i in range(count):
        parts = [grad_a[i * rows_a : (i + 1) * rows_a], grad_b[i * rows_b : (i + 1) * rows_b], blank]
        out_ref[i] = jnp.concatenate(parts, axis=0).astype(BF)


def total_of(ref):
    total = ref[0].astype(F32)
    for i in range(1, ref.shape[0]):
        total = total + ref[i].astype(F32)
    return total


def sum_body(in_ref, out_ref):
    total = total_of(in_ref)
    for i in range(out_ref.shape[0]):
        out_ref[i] = total


def shard_body(moment_a_ref, second_a_ref, moment_b_ref, second_b_ref, moment_ref, second_ref):
    deep, wide = moment_ref.shape
    rank = moment_a_ref.shape[0]
    count = lax.axis_size(PLANE)
    rows_a, rows_b = rank * moment_a_ref.shape[1] // wide // count, rank // count
    place = lax.axis_index(PLANE)
    column = pl.multiple_of(place * rows_a // rank * wide, wide)
    row = pl.multiple_of(lax.rem(place * rows_a, rank), rows_a)
    most = max(rows_b, 8)
    row_b = pl.multiple_of(place * rows_b // most * most, most)

    def piece(a_ref, b_ref):
        of_b = b_ref[pl.ds(row_b, most), :]
        chosen = of_b[:rows_b]
        for i in range(rows_b, most, rows_b):
            chosen = jnp.where(place * rows_b == row_b + i, of_b[i : i + rows_b], chosen)
        pad = jnp.ones((deep - rows_a - rows_b, wide), F32)
        return jnp.concatenate([a_ref[pl.ds(row, rows_a), pl.ds(column, wide)], chosen, pad], axis=0)

    moment_ref[...] = piece(moment_a_ref, moment_b_ref)
    second_ref[...] = piece(second_a_ref, second_b_ref)


def adam_body(in_ref, moment_ref, second_ref, out_ref):
    step = adam_step(total_of(in_ref), moment_ref[...], second_ref[...]).astype(BF)
    for i in range(out_ref.shape[0]):
        out_ref[i] = step


def step_of_a(step_ref, rank, width):
    count, _, wide = step_ref.shape
    rows_a = rank * width // wide // count
    step = jnp.concatenate([step_ref[i].astype(F32)[:rows_a] for i in range(count)], axis=0)
    return unstack(step, rank)


def inner_body(step_ref, a_ref, flat_ref, out_ref):
    rank, width = a_ref.shape
    new_a = (a_ref[...] - learn_rate * step_of_a(step_ref, rank, width)).astype(BF)
    inner = rows_dot(new_a, flat_ref[...]).astype(BF)
    for i in range(out_ref.shape[0]):
        out_ref[i] = inner


def step_body(step_ref, b_ref, step_a_ref, step_b_ref, new_b_ref):
    count = step_ref.shape[0]
    rank, width = step_a_ref.shape
    rows_a, rows_b = rank * width // step_ref.shape[2] // count, rank // count
    step_a_ref[...] = step_of_a(step_ref, rank, width)
    parts = [step_ref[i].astype(F32)[rows_a : rows_a + rows_b] for i in range(count)]
    step_b = jnp.concatenate(parts, axis=0)
    step_b_ref[...] = step_b
    new_b_ref[...] = (b_ref[...] - learn_rate * step_b).astype(BF)


def base_body(value_ref, *refs):
    pieces, out_ref, held, value, copied = refs[:4], *refs[4:]
    core, chip = lax.axis_index("core"), lax.axis_index("zl")
    chips = value.shape[0]
    half = chips // 2
    copies = []
    for i in range(chips):
        place = lax.bitwise_xor(chip, i // half + i % half * half)
        for j in range(2):
            copies.append(
                (
                    pltpu.make_async_copy(
                        pieces[2 * j + i // half].at[i % half], held.at[i, j], copied.at[i, j, 0]
                    ),
                    pltpu.make_async_copy(
                        value_ref.at[place, core if j == 0 else 1 - core], value.at[i, j], copied.at[i, j, 1]
                    ),
                )
            )
    for pair in copies:
        for copy in pair:
            copy.start()
    total = jnp.zeros(out_ref.shape, F32)
    for i in range(chips):
        for j in range(2):
            for copy in copies[2 * i + j]:
                copy.wait()
            total += jnp.dot(held[i, j], value[i, j], preferred_element_type=F32)
    out_ref[...] = total


def cache_body(steps, q_ref, k_ref, v_ref, new_ref, length_ref, out_ref, weight_ref):
    groups, wide = length_ref.shape
    tall = q_ref.shape[0] // groups
    heads = q_ref.shape[1] // HD
    slots = wide // (tall // steps)
    row = lax.broadcasted_iota(jnp.int32, (heads * tall, wide), 0) % tall
    column = lax.broadcasted_iota(jnp.int32, (heads * tall, wide), 1)
    same = row // steps == column // slots
    slot = column % slots
    scale = 1.0 / math.sqrt(HD)
    for g in range(groups):
        query = jnp.concatenate(
            [q_ref[g * tall : (g + 1) * tall, h * HD : (h + 1) * HD] for h in range(heads)], axis=0
        )
        old = rows_dot(query, k_ref[g * wide : (g + 1) * wide, :]) * scale
        old = jnp.where(same & (slot < length_ref[g : g + 1, :]), old, -1e30)
        new = rows_dot(query, new_ref[...]) * scale
        token = column - g * tall
        seen = (token >= 0) & (token < tall) & (token // steps == row // steps) & (token <= row)
        new = jnp.where(seen, new, -1e30)
        largest = jnp.maximum(
            jnp.max(old, axis=1, keepdims=True), jnp.max(new, axis=1, keepdims=True)
        )
        old, new = jnp.exp(old - largest), jnp.exp(new - largest)
        total = jnp.sum(old, axis=1, keepdims=True) + jnp.sum(new, axis=1, keepdims=True)
        at = slice(g * heads * tall, (g + 1) * heads * tall)
        weight_ref[at, :] = (new / total).astype(BF)
        out_ref[at, :] = jnp.dot(
            (old / total).astype(BF), v_ref[g * wide : (g + 1) * wide, :], preferred_element_type=F32
        )


def last_body(groups, inner_ref, new_b_ref, base_ref, old_ref, weight_ref, out_ref):
    inner = total_of(inner_ref).astype(BF)
    change = columns_dot(inner, new_b_ref[...])
    values = (base_ref[...] + adapter_scale * change).astype(BF)
    rows, steps, wide = out_ref.shape
    each = rows // groups
    tall = each * steps
    heads = wide // HD
    for g in range(groups):
        at = slice(g * heads * tall, (g + 1) * heads * tall)
        out = old_ref[at, :] + jnp.dot(weight_ref[at, :], values, preferred_element_type=F32)
        for h in range(heads):
            part = out[h * tall : (h + 1) * tall].reshape(each, steps, HD)
            out_ref[g * each : (g + 1) * each, :, h * HD : (h + 1) * HD] = part.astype(BF)


def local(
    trainer_token_input,
    cotangent,
    adapter_a,
    adapter_b,
    moment_a,
    second_a,
    moment_b,
    second_b,
    value_matrix,
    decode_states,
    new_keys,
    queries,
    cache_keys,
    cache_values,
    lengths,
):
    pairs = lax.axis_size("zl")
    tensor = lax.axis_size(TENSOR)
    plane = lax.axis_size(PLANE)
    tokens, width = trainer_token_input.shape
    rank = adapter_a.shape[1]
    kv = cotangent.shape[1]
    rows, steps, _ = decode_states.shape
    count = rows * steps
    slots = cache_keys.shape[1]
    two = 2 * rank
    flat = lax.optimization_barrier(decode_states.reshape(count, width))
    a_turned = adapter_a.T

    half = shape((tokens // 2, two), F32)
    starts = (trainer_token_input, cotangent, a_turned, adapter_b)
    mine, theirs = call(low_body, (half, half), *map(far, starts))
    pair = call(pair_body, shape((pairs, tokens // 2, two), BF), mine, swap(theirs))

    pair, send = lax.optimization_barrier((pair, flat))
    second_chip = reach(send[None], 2)
    mine = jnp.sum(trade(pair, "zl").astype(F32), axis=0).astype(BF)
    mine, moments = lax.optimization_barrier((mine, (moment_a.T, second_a.T, moment_b, second_b)))
    theirs = swap(mine)
    rows_a, rows_b = rank * width // kv // plane, rank // plane
    deep = rows_a + rows_b + -(rows_a + rows_b) % 16
    piece = shape((deep, kv), F32)
    moments = call(shard_body, (piece, piece), *map(far, moments))
    theirs, moments = lax.optimization_barrier((theirs, moments))

    scale = adapter_scale / (tokens * lax.axis_size(DP))
    block = call(
        lambda *refs: gradient_body(scale, *refs),
        shape((plane, deep, kv), BF),
        trainer_token_input,
        cotangent,
        mine,
        theirs,
    )

    shard = trade(block, PLANE)
    near = jnp.concatenate([send[None], second_chip], axis=0)
    distant = reach(near, 1)
    shard = call(sum_body, shape((lax.axis_size("zh"), deep, kv), F32), shard)
    shard, query = lax.optimization_barrier((shard, queries))
    shard = trade(shard, "zh")

    groups = rows * slots // HD
    heads = queries.shape[2] // HD
    old, weights = call(
        lambda *refs: cache_body(steps, *refs),
        (shape((count * heads, HD), F32), shape((count * heads, count), BF)),
        query.reshape(count, heads * HD),
        cache_keys.reshape(rows * slots, kv),
        cache_values.reshape(rows * slots, kv),
        new_keys.reshape(count, kv),
        jnp.repeat(lengths, slots).reshape(groups, HD),
        flops=2 * count * heads * HD * HD * 3,
        moved=8 * 2**20,
    )
    shard, old, weights = lax.optimization_barrier((shard, old, weights))
    step = call(adam_body, shape((plane, deep, kv), BF), shard, *moments)
    distant_sent, near_sent, _ = lax.optimization_barrier((distant, near, step))
    distant_other, near_other = swap(distant_sent), swap(near_sent)
    step = trade(step, PLANE)

    inner = call(inner_body, shape((tensor, rank, count), BF), step, a_turned, flat)
    inner = trade(inner, TENSOR)
    step_a, step_b, new_b = call(
        step_body, (shape((rank, width), F32), shape((rank, kv), F32), shape((rank, kv), BF)), step, adapter_b
    )
    base = call(
        base_body,
        shape((count, kv), F32),
        far(value_matrix.reshape(pairs, 2, width, kv)),
        near,
        distant,
        near_other,
        distant_other,
        flops=2 * count * tensor * width * kv,
        moved=4 * 2**20,
        in_specs=[pl.BlockSpec(memory_space=pl.ANY)] * 5,
        scratch_shapes=[
            pltpu.VMEM((pairs, 2, count, width), BF),
            pltpu.VMEM((pairs, 2, width, kv), BF),
            pltpu.SemaphoreType.DMA((pairs, 2, 2)),
        ],
    )

    attended = call(
        lambda *refs: last_body(groups, *refs),
        shape((rows, steps, heads * HD), BF),
        inner,
        new_b,
        base,
        old,
        weights,
    )
    return (step_a.T, step_b, attended)


def solution(mesh):
    sizes = (4, 4, 4, mesh.devices.shape[1] // 2, 2)
    fine = Mesh(mesh.devices.reshape(sizes), DP + TENSOR)
    return jax.shard_map(
        local,
        mesh=fine,
        in_specs=(
            P(DP, TENSOR),
            P(DP, TENSOR),
            P(TENSOR, None),
            P(None, TENSOR),
            P(TENSOR, None),
            P(TENSOR, None),
            P(None, TENSOR),
            P(None, TENSOR),
            P(None, TENSOR),
            P(DP, None, TENSOR),
            P(DP, None, TENSOR),
            P(DP, None, TENSOR),
            P(DP, None, TENSOR),
            P(DP, None, TENSOR),
            P(DP),
        ),
        out_specs=(P(TENSOR, None), P(None, TENSOR), P(DP, None, TENSOR)),
        check_vma=False,
    )
```

```python
import math

import jax
import jax.numpy as jnp
from jax import lax
from jax.experimental import pallas as pl
from jax.experimental.pallas import tpu as pltpu
from jax.sharding import Mesh, PartitionSpec as P

HD = 128


adapter_scale = 2.0
learn_rate = 0.001
beta_one = 0.9
beta_two = 0.999
adam_eps = 1e-08
first_fix = 1.0 - 0.9**10
second_fix = 1.0 - 0.999**10

DP = ("x", "zh", "y")
PLANE = ("x", "y")
TENSOR = ("zl", "core")
BF = jnp.bfloat16
F32 = jnp.float32


def adam_step(grad, moment, second):
    moment_new = beta_one * moment + (1.0 - beta_one) * grad
    second_new = beta_two * second + (1.0 - beta_two) * grad * grad
    return moment_new / first_fix / (jnp.sqrt(second_new / second_fix) + adam_eps)


def trade(parts, axes):
    return lax.all_to_all(parts, axes, 0, 0, tiled=True)


def swap(value):
    return lax.ppermute(value, "core", [(0, 1), (1, 0)])


def reach(value, hop):
    return lax.ppermute(value, "zl", [(i, i ^ hop) for i in range(lax.axis_size("zl"))])


def call(body, out, *args, flops=0, moved=0, **more):
    return pl.pallas_call(
        body,
        out_shape=out,
        cost_estimate=pl.CostEstimate(flops=flops, bytes_accessed=moved, transcendentals=0),
        compiler_params=pltpu.CompilerParams(vmem_limit_bytes=16 * 2**20),
        **more,
    )(*args)


def far(value):
    return pltpu.with_memory_space_constraint(value, pltpu.HBM)


def shape(dims, kind):
    return jax.ShapeDtypeStruct(dims, kind)


def columns_dot(a, b):
    return lax.dot_general(a, b, (((0,), (0,)), ((), ())), preferred_element_type=F32)


def rows_dot(a, b):
    return lax.dot_general(a, b, (((1,), (1,)), ((), ())), preferred_element_type=F32)


def low_body(x_ref, cot_ref, a_ref, b_ref, mine_ref, theirs_ref):
    acts = rows_dot(x_ref[...], a_ref[...].astype(BF))
    grads = rows_dot(cot_ref[...], b_ref[...].astype(BF))
    both = jnp.concatenate([acts, grads], axis=1)
    half = both.shape[0] // 2
    first = lax.axis_index("core") == 0
    mine_ref[...] = jnp.where(first, both[:half], both[half:])
    theirs_ref[...] = jnp.where(first, both[half:], both[:half])


def pair_body(mine_ref, theirs_ref, out_ref):
    total = (mine_ref[...] + theirs_ref[...]).astype(BF)
    for i in range(out_ref.shape[0]):
        out_ref[i] = total


def stack(value, wide):
    return jnp.concatenate([value[:, i : i + wide] for i in range(0, value.shape[1], wide)], axis=0)


def unstack(value, tall):
    return jnp.concatenate([value[i : i + tall] for i in range(0, value.shape[0], tall)], axis=1)


def gradient_body(scale, x_ref, cot_ref, mine_ref, theirs_ref, out_ref):
    mine, theirs = mine_ref[...].astype(F32), theirs_ref[...].astype(F32)
    first = lax.axis_index("core") == 0
    low = jnp.concatenate([jnp.where(first, mine, theirs), jnp.where(first, theirs, mine)], axis=0)
    rank = low.shape[1] // 2
    low = low.astype(BF)
    count, deep, wide = out_ref.shape
    grad_a = stack(columns_dot(low, x_ref[...])[rank:], wide) * scale
    grad_b = columns_dot(low, cot_ref[...])[:rank] * scale
    rows_a, rows_b = grad_a.shape[0] // count, rank // count
    blank = jnp.zeros((deep - rows_a - rows_b, wide), F32)
    for i in range(count):
        parts = [grad_a[i * rows_a : (i + 1) * rows_a], grad_b[i * rows_b : (i + 1) * rows_b], blank]
        out_ref[i] = jnp.concatenate(parts, axis=0).astype(BF)


def total_of(ref):
    total = ref[0].astype(F32)
    for i in range(1, ref.shape[0]):
        total = total + ref[i].astype(F32)
    return total


def sum_body(in_ref, out_ref):
    total = total_of(in_ref)
    for i in range(out_ref.shape[0]):
        out_ref[i] = total


def shard_body(moment_a_ref, second_a_ref, moment_b_ref, second_b_ref, moment_ref, second_ref):
    deep, wide = moment_ref.shape
    rank = moment_a_ref.shape[0]
    count = lax.axis_size(PLANE)
    rows_a, rows_b = rank * moment_a_ref.shape[1] // wide // count, rank // count
    place = lax.axis_index(PLANE)
    column = pl.multiple_of(place * rows_a // rank * wide, wide)
    row = pl.multiple_of(lax.rem(place * rows_a, rank), rows_a)
    most = max(rows_b, 8)
    row_b = pl.multiple_of(place * rows_b // most * most, most)

    def piece(a_ref, b_ref):
        of_b = b_ref[pl.ds(row_b, most), :]
        chosen = of_b[:rows_b]
        for i in range(rows_b, most, rows_b):
            chosen = jnp.where(place * rows_b == row_b + i, of_b[i : i + rows_b], chosen)
        pad = jnp.ones((deep - rows_a - rows_b, wide), F32)
        return jnp.concatenate([a_ref[pl.ds(row, rows_a), pl.ds(column, wide)], chosen, pad], axis=0)

    moment_ref[...] = piece(moment_a_ref, moment_b_ref)
    second_ref[...] = piece(second_a_ref, second_b_ref)


def adam_body(in_ref, moment_ref, second_ref, out_ref):
    step = adam_step(total_of(in_ref), moment_ref[...], second_ref[...]).astype(BF)
    for i in range(out_ref.shape[0]):
        out_ref[i] = step


def step_of_a(step_ref, rank, width):
    count, _, wide = step_ref.shape
    rows_a = rank * width // wide // count
    step = jnp.concatenate([step_ref[i].astype(F32)[:rows_a] for i in range(count)], axis=0)
    return unstack(step, rank)


def inner_body(step_ref, a_ref, flat_ref, out_ref):
    rank, width = a_ref.shape
    new_a = (a_ref[...] - learn_rate * step_of_a(step_ref, rank, width)).astype(BF)
    inner = rows_dot(new_a, flat_ref[...]).astype(BF)
    for i in range(out_ref.shape[0]):
        out_ref[i] = inner


def step_body(step_ref, b_ref, step_a_ref, step_b_ref, new_b_ref):
    count = step_ref.shape[0]
    rank, width = step_a_ref.shape
    rows_a, rows_b = rank * width // step_ref.shape[2] // count, rank // count
    step_a_ref[...] = step_of_a(step_ref, rank, width)
    parts = [step_ref[i].astype(F32)[rows_a : rows_a + rows_b] for i in range(count)]
    step_b = jnp.concatenate(parts, axis=0)
    step_b_ref[...] = step_b
    new_b_ref[...] = (b_ref[...] - learn_rate * step_b).astype(BF)


def base_body(value_ref, *refs):
    pieces, out_ref, held, value, copied = refs[:4], *refs[4:]
    core, chip = lax.axis_index("core"), lax.axis_index("zl")
    chips = value.shape[0]
    half = chips // 2
    copies = []
    for i in range(chips):
        place = lax.bitwise_xor(chip, i // half + i % half * half)
        for j in range(2):
            copies.append(
                (
                    pltpu.make_async_copy(
                        pieces[2 * j + i // half].at[i % half], held.at[i, j], copied.at[i, j, 0]
                    ),
                    pltpu.make_async_copy(
                        value_ref.at[place, core if j == 0 else 1 - core], value.at[i, j], copied.at[i, j, 1]
                    ),
                )
            )
    for pair in copies:
        for copy in pair:
            copy.start()
    total = jnp.zeros(out_ref.shape, F32)
    for i in range(chips):
        for j in range(2):
            for copy in copies[2 * i + j]:
                copy.wait()
            total += jnp.dot(held[i, j], value[i, j], preferred_element_type=F32)
    out_ref[...] = total


def cache_body(steps, q_ref, k_ref, v_ref, new_ref, length_ref, out_ref, weight_ref):
    groups, wide = length_ref.shape
    tall = q_ref.shape[0] // groups
    heads = q_ref.shape[1] // HD
    slots = wide // (tall // steps)
    row = lax.broadcasted_iota(jnp.int32, (heads * tall, wide), 0) % tall
    column = lax.broadcasted_iota(jnp.int32, (heads * tall, wide), 1)
    same = row // steps == column // slots
    slot = column % slots
    scale = 1.0 / math.sqrt(HD)
    for g in range(groups):
        query = jnp.concatenate(
            [q_ref[g * tall : (g + 1) * tall, h * HD : (h + 1) * HD] for h in range(heads)], axis=0
        )
        old = rows_dot(query, k_ref[g * wide : (g + 1) * wide, :]) * scale
        old = jnp.where(same & (slot < length_ref[g : g + 1, :]), old, -1e30)
        new = rows_dot(query, new_ref[...]) * scale
        token = column - g * tall
        seen = (token >= 0) & (token < tall) & (token // steps == row // steps) & (token <= row)
        new = jnp.where(seen, new, -1e30)
        largest = jnp.maximum(
            jnp.max(old, axis=1, keepdims=True), jnp.max(new, axis=1, keepdims=True)
        )
        old, new = jnp.exp(old - largest), jnp.exp(new - largest)
        total = jnp.sum(old, axis=1, keepdims=True) + jnp.sum(new, axis=1, keepdims=True)
        at = slice(g * heads * tall, (g + 1) * heads * tall)
        weight_ref[at, :] = (new / total).astype(BF)
        out_ref[at, :] = jnp.dot(
            (old / total).astype(BF), v_ref[g * wide : (g + 1) * wide, :], preferred_element_type=F32
        )


def last_body(groups, inner_ref, new_b_ref, base_ref, old_ref, weight_ref, out_ref):
    inner = total_of(inner_ref).astype(BF)
    change = columns_dot(inner, new_b_ref[...])
    values = (base_ref[...] + adapter_scale * change).astype(BF)
    rows, steps, wide = out_ref.shape
    each = rows // groups
    tall = each * steps
    heads = wide // HD
    for g in range(groups):
        at = slice(g * heads * tall, (g + 1) * heads * tall)
        out = old_ref[at, :] + jnp.dot(weight_ref[at, :], values, preferred_element_type=F32)
        for h in range(heads):
            part = out[h * tall : (h + 1) * tall].reshape(each, steps, HD)
            out_ref[g * each : (g + 1) * each, :, h * HD : (h + 1) * HD] = part.astype(BF)


def local(
    trainer_token_input,
    cotangent,
    adapter_a,
    adapter_b,
    moment_a,
    second_a,
    moment_b,
    second_b,
    value_matrix,
    decode_states,
    new_keys,
    queries,
    cache_keys,
    cache_values,
    lengths,
):
    pairs = lax.axis_size("zl")
    tensor = lax.axis_size(TENSOR)
    plane = lax.axis_size(PLANE)
    tokens, width = trainer_token_input.shape
    rank = adapter_a.shape[1]
    kv = cotangent.shape[1]
    rows, steps, _ = decode_states.shape
    count = rows * steps
    slots = cache_keys.shape[1]
    two = 2 * rank
    flat = lax.optimization_barrier(decode_states.reshape(count, width))
    a_turned = adapter_a.T

    second_chip = reach(decode_states, 2)

    half = shape((tokens // 2, two), F32)
    starts = (trainer_token_input, cotangent, a_turned, adapter_b)
    mine, theirs = call(low_body, (half, half), *map(far, starts))
    pair = call(pair_body, shape((pairs, tokens // 2, two), BF), mine, swap(theirs))

    mine = jnp.sum(trade(pair, "zl").astype(F32), axis=0).astype(BF)
    mine, moments = lax.optimization_barrier((mine, (moment_a.T, second_a.T, moment_b, second_b)))
    theirs = swap(mine)
    rows_a, rows_b = rank * width // kv // plane, rank // plane
    deep = rows_a + rows_b + -(rows_a + rows_b) % 16
    piece = shape((deep, kv), F32)
    moments = call(shard_body, (piece, piece), *map(far, moments))
    theirs, moments = lax.optimization_barrier((theirs, moments))

    scale = adapter_scale / (tokens * lax.axis_size(DP))
    block = call(
        lambda *refs: gradient_body(scale, *refs),
        shape((plane, deep, kv), BF),
        trainer_token_input,
        cotangent,
        mine,
        theirs,
    )

    shard = trade(block, PLANE)
    near = jnp.stack([flat, second_chip.reshape(count, width)])
    distant = reach(near, 1)
    shard = call(sum_body, shape((lax.axis_size("zh"), deep, kv), F32), shard)
    shard, query = lax.optimization_barrier((shard, queries))
    shard = trade(shard, "zh")

    groups = rows * slots // HD
    heads = queries.shape[2] // HD
    old, weights = call(
        lambda *refs: cache_body(steps, *refs),
        (shape((count * heads, HD), F32), shape((count * heads, count), BF)),
        query.reshape(count, heads * HD),
        cache_keys.reshape(rows * slots, kv),
        cache_values.reshape(rows * slots, kv),
        new_keys.reshape(count, kv),
        jnp.repeat(lengths, slots).reshape(groups, HD),
        flops=2 * count * heads * HD * HD * 3,
        moved=8 * 2**20,
    )
    shard, old, weights = lax.optimization_barrier((shard, old, weights))
    step = call(adam_body, shape((plane, deep, kv), BF), shard, *moments)
    distant_other, near_other = swap(distant), swap(near)
    step = trade(step, PLANE)

    base = call(
        base_body,
        shape((count, kv), F32),
        far(value_matrix.reshape(pairs, 2, width, kv)),
        near,
        distant,
        near_other,
        distant_other,
        flops=2 * count * tensor * width * kv,
        moved=4 * 2**20,
        in_specs=[pl.BlockSpec(memory_space=pl.ANY)] * 5,
        scratch_shapes=[
            pltpu.VMEM((pairs, 2, count, width), BF),
            pltpu.VMEM((pairs, 2, width, kv), BF),
            pltpu.SemaphoreType.DMA((pairs, 2, 2)),
        ],
    )

    step, base = lax.optimization_barrier((step, base))

    inner = call(inner_body, shape((tensor, rank, count), BF), step, a_turned, flat)
    inner = trade(inner, TENSOR)
    step_a, step_b, new_b = call(
        step_body, (shape((rank, width), F32), shape((rank, kv), F32), shape((rank, kv), BF)), step, adapter_b
    )

    attended = call(
        lambda *refs: last_body(groups, *refs),
        shape((rows, steps, heads * HD), BF),
        inner,
        new_b,
        base,
        old,
        weights,
    )
    return (step_a.T, step_b, attended)


def solution(mesh):
    sizes = (4, 4, 4, mesh.devices.shape[1] // 2, 2)
    fine = Mesh(mesh.devices.reshape(sizes), DP + TENSOR)
    return jax.shard_map(
        local,
        mesh=fine,
        in_specs=(
            P(DP, TENSOR),
            P(DP, TENSOR),
            P(TENSOR, None),
            P(None, TENSOR),
            P(TENSOR, None),
            P(TENSOR, None),
            P(None, TENSOR),
            P(None, TENSOR),
            P(None, TENSOR),
            P(DP, None, TENSOR),
            P(DP, None, TENSOR),
            P(DP, None, TENSOR),
            P(DP, None, TENSOR),
            P(DP, None, TENSOR),
            P(DP),
        ),
        out_specs=(P(TENSOR, None), P(None, TENSOR), P(DP, None, TENSOR)),
        check_vma=False,
    )
```

```python
import math

import jax
import jax.numpy as jnp
from jax import lax
from jax.experimental import pallas as pl
from jax.experimental.pallas import tpu as pltpu
from jax.sharding import Mesh, PartitionSpec as P

HD = 128


adapter_scale = 2.0
learn_rate = 0.001
beta_one = 0.9
beta_two = 0.999
adam_eps = 1e-08
first_fix = 1.0 - 0.9**10
second_fix = 1.0 - 0.999**10

DP = ("x", "zh", "y")
PLANE = ("x", "y")
TENSOR = ("zl", "core")
BF = jnp.bfloat16
F32 = jnp.float32


def adam_step(grad, moment, second):
    moment_new = beta_one * moment + (1.0 - beta_one) * grad
    second_new = beta_two * second + (1.0 - beta_two) * grad * grad
    return moment_new / first_fix / (jnp.sqrt(second_new / second_fix) + adam_eps)


def trade(parts, axes):
    return lax.all_to_all(parts, axes, 0, 0, tiled=True)


def swap(value):
    return lax.ppermute(value, "core", [(0, 1), (1, 0)])


def reach(value, hop):
    return lax.ppermute(value, "zl", [(i, i ^ hop) for i in range(lax.axis_size("zl"))])


def call(body, out, *args, flops=0, moved=0, **more):
    return pl.pallas_call(
        body,
        out_shape=out,
        cost_estimate=pl.CostEstimate(flops=flops, bytes_accessed=moved, transcendentals=0),
        compiler_params=pltpu.CompilerParams(vmem_limit_bytes=16 * 2**20),
        **more,
    )(*args)


def far(value):
    return pltpu.with_memory_space_constraint(value, pltpu.HBM)


def shape(dims, kind):
    return jax.ShapeDtypeStruct(dims, kind)


def columns_dot(a, b):
    return lax.dot_general(a, b, (((0,), (0,)), ((), ())), preferred_element_type=F32)


def rows_dot(a, b):
    return lax.dot_general(a, b, (((1,), (1,)), ((), ())), preferred_element_type=F32)


def low_body(x_ref, cot_ref, a_ref, b_ref, mine_ref, theirs_ref):
    acts = rows_dot(x_ref[...], a_ref[...].astype(BF))
    grads = rows_dot(cot_ref[...], b_ref[...].astype(BF))
    both = jnp.concatenate([acts, grads], axis=1)
    half = both.shape[0] // 2
    first = lax.axis_index("core") == 0
    mine_ref[...] = jnp.where(first, both[:half], both[half:])
    theirs_ref[...] = jnp.where(first, both[half:], both[:half])


def pair_body(mine_ref, theirs_ref, out_ref):
    total = (mine_ref[...] + theirs_ref[...]).astype(BF)
    for i in range(out_ref.shape[0]):
        out_ref[i] = total


def stack(value, wide):
    return jnp.concatenate([value[:, i : i + wide] for i in range(0, value.shape[1], wide)], axis=0)


def unstack(value, tall):
    return jnp.concatenate([value[i : i + tall] for i in range(0, value.shape[0], tall)], axis=1)


def gradient_body(scale, x_ref, cot_ref, mine_ref, theirs_ref, out_ref):
    mine, theirs = mine_ref[...].astype(F32), theirs_ref[...].astype(F32)
    first = lax.axis_index("core") == 0
    low = jnp.concatenate([jnp.where(first, mine, theirs), jnp.where(first, theirs, mine)], axis=0)
    rank = low.shape[1] // 2
    low = low.astype(BF)
    count, deep, wide = out_ref.shape
    grad_a = stack(columns_dot(low, x_ref[...])[rank:], wide) * scale
    grad_b = columns_dot(low, cot_ref[...])[:rank] * scale
    rows_a, rows_b = grad_a.shape[0] // count, rank // count
    blank = jnp.zeros((deep - rows_a - rows_b, wide), F32)
    for i in range(count):
        parts = [grad_a[i * rows_a : (i + 1) * rows_a], grad_b[i * rows_b : (i + 1) * rows_b], blank]
        out_ref[i] = jnp.concatenate(parts, axis=0).astype(BF)


def total_of(ref):
    total = ref[0].astype(F32)
    for i in range(1, ref.shape[0]):
        total = total + ref[i].astype(F32)
    return total


def sum_body(in_ref, out_ref):
    total = total_of(in_ref).astype(BF)
    for i in range(out_ref.shape[0]):
        out_ref[i] = total


def shard_body(moment_a_ref, second_a_ref, moment_b_ref, second_b_ref, moment_ref, second_ref):
    deep, wide = moment_ref.shape
    rank = moment_a_ref.shape[0]
    count = lax.axis_size(PLANE)
    rows_a, rows_b = rank * moment_a_ref.shape[1] // wide // count, rank // count
    place = lax.axis_index(PLANE)
    column = pl.multiple_of(place * rows_a // rank * wide, wide)
    row = pl.multiple_of(lax.rem(place * rows_a, rank), rows_a)
    most = max(rows_b, 8)
    row_b = pl.multiple_of(place * rows_b // most * most, most)

    def piece(a_ref, b_ref):
        of_b = b_ref[pl.ds(row_b, most), :]
        chosen = of_b[:rows_b]
        for i in range(rows_b, most, rows_b):
            chosen = jnp.where(place * rows_b == row_b + i, of_b[i : i + rows_b], chosen)
        pad = jnp.ones((deep - rows_a - rows_b, wide), F32)
        return jnp.concatenate([a_ref[pl.ds(row, rows_a), pl.ds(column, wide)], chosen, pad], axis=0)

    moment_ref[...] = piece(moment_a_ref, moment_b_ref)
    second_ref[...] = piece(second_a_ref, second_b_ref)


def adam_body(in_ref, moment_ref, second_ref, out_ref):
    step = adam_step(total_of(in_ref), moment_ref[...], second_ref[...]).astype(BF)
    for i in range(out_ref.shape[0]):
        out_ref[i] = step


def step_of_a(step_ref, rank, width):
    count, _, wide = step_ref.shape
    rows_a = rank * width // wide // count
    step = jnp.concatenate([step_ref[i].astype(F32)[:rows_a] for i in range(count)], axis=0)
    return unstack(step, rank)


def inner_body(step_ref, a_ref, flat_ref, out_ref):
    rank, width = a_ref.shape
    new_a = (a_ref[...] - learn_rate * step_of_a(step_ref, rank, width)).astype(BF)
    inner = rows_dot(new_a, flat_ref[...]).astype(BF)
    for i in range(out_ref.shape[0]):
        out_ref[i] = inner


def step_body(step_ref, b_ref, step_a_ref, step_b_ref, new_b_ref):
    count = step_ref.shape[0]
    rank, width = step_a_ref.shape
    rows_a, rows_b = rank * width // step_ref.shape[2] // count, rank // count
    step_a_ref[...] = step_of_a(step_ref, rank, width)
    parts = [step_ref[i].astype(F32)[rows_a : rows_a + rows_b] for i in range(count)]
    step_b = jnp.concatenate(parts, axis=0)
    step_b_ref[...] = step_b
    new_b_ref[...] = (b_ref[...] - learn_rate * step_b).astype(BF)


def base_body(value_ref, *refs):
    pieces, out_ref, held, value, copied = refs[:4], *refs[4:]
    core, chip = lax.axis_index("core"), lax.axis_index("zl")
    chips = value.shape[0]
    half = chips // 2
    copies = []
    for i in range(chips):
        place = lax.bitwise_xor(chip, i // half + i % half * half)
        for j in range(2):
            copies.append(
                (
                    pltpu.make_async_copy(
                        pieces[2 * j + i // half].at[i % half], held.at[i, j], copied.at[i, j, 0]
                    ),
                    pltpu.make_async_copy(
                        value_ref.at[place, core if j == 0 else 1 - core], value.at[i, j], copied.at[i, j, 1]
                    ),
                )
            )
    for pair in copies:
        for copy in pair:
            copy.start()
    total = jnp.zeros(out_ref.shape, F32)
    for i in range(chips):
        for j in range(2):
            for copy in copies[2 * i + j]:
                copy.wait()
            total += jnp.dot(held[i, j], value[i, j], preferred_element_type=F32)
    out_ref[...] = total


def cache_body(steps, q_ref, k_ref, v_ref, new_ref, length_ref, out_ref, weight_ref):
    groups, wide = length_ref.shape
    tall = q_ref.shape[0] // groups
    heads = q_ref.shape[1] // HD
    slots = wide // (tall // steps)
    row = lax.broadcasted_iota(jnp.int32, (heads * tall, wide), 0) % tall
    column = lax.broadcasted_iota(jnp.int32, (heads * tall, wide), 1)
    same = row // steps == column // slots
    slot = column % slots
    scale = 1.0 / math.sqrt(HD)
    for g in range(groups):
        query = jnp.concatenate(
            [q_ref[g * tall : (g + 1) * tall, h * HD : (h + 1) * HD] for h in range(heads)], axis=0
        )
        old = rows_dot(query, k_ref[g * wide : (g + 1) * wide, :]) * scale
        old = jnp.where(same & (slot < length_ref[g : g + 1, :]), old, -1e30)
        new = rows_dot(query, new_ref[...]) * scale
        token = column - g * tall
        seen = (token >= 0) & (token < tall) & (token // steps == row // steps) & (token <= row)
        new = jnp.where(seen, new, -1e30)
        largest = jnp.maximum(
            jnp.max(old, axis=1, keepdims=True), jnp.max(new, axis=1, keepdims=True)
        )
        old, new = jnp.exp(old - largest), jnp.exp(new - largest)
        total = jnp.sum(old, axis=1, keepdims=True) + jnp.sum(new, axis=1, keepdims=True)
        at = slice(g * heads * tall, (g + 1) * heads * tall)
        weight_ref[at, :] = (new / total).astype(BF)
        out_ref[at, :] = jnp.dot(
            (old / total).astype(BF), v_ref[g * wide : (g + 1) * wide, :], preferred_element_type=F32
        )


def last_body(groups, inner_ref, new_b_ref, base_ref, old_ref, weight_ref, out_ref):
    inner = total_of(inner_ref).astype(BF)
    change = columns_dot(inner, new_b_ref[...])
    values = (base_ref[...] + adapter_scale * change).astype(BF)
    rows, steps, wide = out_ref.shape
    each = rows // groups
    tall = each * steps
    heads = wide // HD
    for g in range(groups):
        at = slice(g * heads * tall, (g + 1) * heads * tall)
        out = old_ref[at, :] + jnp.dot(weight_ref[at, :], values, preferred_element_type=F32)
        for h in range(heads):
            part = out[h * tall : (h + 1) * tall].reshape(each, steps, HD)
            out_ref[g * each : (g + 1) * each, :, h * HD : (h + 1) * HD] = part.astype(BF)


def local(
    trainer_token_input,
    cotangent,
    adapter_a,
    adapter_b,
    moment_a,
    second_a,
    moment_b,
    second_b,
    value_matrix,
    decode_states,
    new_keys,
    queries,
    cache_keys,
    cache_values,
    lengths,
):
    pairs = lax.axis_size("zl")
    tensor = lax.axis_size(TENSOR)
    plane = lax.axis_size(PLANE)
    tokens, width = trainer_token_input.shape
    rank = adapter_a.shape[1]
    kv = cotangent.shape[1]
    rows, steps, _ = decode_states.shape
    count = rows * steps
    slots = cache_keys.shape[1]
    two = 2 * rank
    flat = lax.optimization_barrier(decode_states.reshape(count, width))
    a_turned = adapter_a.T

    half = shape((tokens // 2, two), F32)
    starts = (trainer_token_input, cotangent, a_turned, adapter_b)
    mine, theirs = call(low_body, (half, half), *map(far, starts))
    pair = call(pair_body, shape((pairs, tokens // 2, two), BF), mine, swap(theirs))

    pair, send = lax.optimization_barrier((pair, flat))
    second_chip = reach(send[None], 2)
    mine = jnp.sum(trade(pair, "zl").astype(F32), axis=0).astype(BF)
    mine, moments = lax.optimization_barrier((mine, (moment_a.T, second_a.T, moment_b, second_b)))
    theirs = swap(mine)
    rows_a, rows_b = rank * width // kv // plane, rank // plane
    deep = rows_a + rows_b + -(rows_a + rows_b) % 8
    piece = shape((deep, kv), F32)
    moments = call(shard_body, (piece, piece), *map(far, moments))
    theirs, moments = lax.optimization_barrier((theirs, moments))

    scale = adapter_scale / (tokens * lax.axis_size(DP))
    block = call(
        lambda *refs: gradient_body(scale, *refs),
        shape((plane, deep, kv), BF),
        trainer_token_input,
        cotangent,
        mine,
        theirs,
    )

    block, query = lax.optimization_barrier((block, queries))
    shard = trade(block, PLANE)

    groups = rows * slots // HD
    heads = queries.shape[2] // HD
    old, weights = call(
        lambda *refs: cache_body(steps, *refs),
        (shape((count * heads, HD), F32), shape((count * heads, count), BF)),
        query.reshape(count, heads * HD),
        cache_keys.reshape(rows * slots, kv),
        cache_values.reshape(rows * slots, kv),
        new_keys.reshape(count, kv),
        jnp.repeat(lengths, slots).reshape(groups, HD),
        flops=2 * count * heads * HD * HD * 3,
        moved=8 * 2**20,
    )
    shard, old, weights = lax.optimization_barrier((shard, old, weights))
    near = jnp.concatenate([send[None], second_chip], axis=0)
    distant = reach(near, 1)
    shard = call(sum_body, shape((lax.axis_size("zh"), deep, kv), BF), shard)
    shard = trade(shard, "zh")

    step = adam_step(jnp.sum(shard.astype(F32), axis=0), *moments).astype(BF)
    step = jnp.broadcast_to(step[None], (plane, deep, kv))
    distant_sent, near_sent, _ = lax.optimization_barrier((distant, near, step))
    distant_other, near_other = swap(distant_sent), swap(near_sent)
    step = trade(step, PLANE)

    inner = call(inner_body, shape((tensor, rank, count), BF), step, a_turned, flat)
    inner = trade(inner, TENSOR)
    step_a, step_b, new_b = call(
        step_body, (shape((rank, width), F32), shape((rank, kv), F32), shape((rank, kv), BF)), step, adapter_b
    )
    base = call(
        base_body,
        shape((count, kv), F32),
        far(value_matrix.reshape(pairs, 2, width, kv)),
        near,
        distant,
        near_other,
        distant_other,
        flops=2 * count * tensor * width * kv,
        moved=4 * 2**20,
        in_specs=[pl.BlockSpec(memory_space=pl.ANY)] * 5,
        scratch_shapes=[
            pltpu.VMEM((pairs, 2, count, width), BF),
            pltpu.VMEM((pairs, 2, width, kv), BF),
            pltpu.SemaphoreType.DMA((pairs, 2, 2)),
        ],
    )

    attended = call(
        lambda *refs: last_body(groups, *refs),
        shape((rows, steps, heads * HD), BF),
        inner,
        new_b,
        base,
        old,
        weights,
    )
    return (step_a.T, step_b, attended)


def solution(mesh):
    sizes = (4, 4, 4, mesh.devices.shape[1] // 2, 2)
    fine = Mesh(mesh.devices.reshape(sizes), DP + TENSOR)
    return jax.shard_map(
        local,
        mesh=fine,
        in_specs=(
            P(DP, TENSOR),
            P(DP, TENSOR),
            P(TENSOR, None),
            P(None, TENSOR),
            P(TENSOR, None),
            P(TENSOR, None),
            P(None, TENSOR),
            P(None, TENSOR),
            P(None, TENSOR),
            P(DP, None, TENSOR),
            P(DP, None, TENSOR),
            P(DP, None, TENSOR),
            P(DP, None, TENSOR),
            P(DP, None, TENSOR),
            P(DP),
        ),
        out_specs=(P(TENSOR, None), P(None, TENSOR), P(DP, None, TENSOR)),
        check_vma=False,
    )
```

```python
import math

import jax
import jax.numpy as jnp
from jax import lax
from jax.experimental import pallas as pl
from jax.experimental.pallas import tpu as pltpu
from jax.sharding import Mesh, PartitionSpec as P

HD = 128


adapter_scale = 2.0
learn_rate = 0.001
beta_one = 0.9
beta_two = 0.999
adam_eps = 1e-08
first_fix = 1.0 - 0.9**10
second_fix = 1.0 - 0.999**10

DP = ("x", "zh", "y")
PLANE = ("x", "y")
TENSOR = ("zl", "core")
BF = jnp.bfloat16
F32 = jnp.float32


def adam_step(grad, moment, second):
    moment_new = beta_one * moment + (1.0 - beta_one) * grad
    second_new = beta_two * second + (1.0 - beta_two) * grad * grad
    return moment_new / first_fix / (jnp.sqrt(second_new / second_fix) + adam_eps)


def trade(parts, axes):
    return lax.all_to_all(parts, axes, 0, 0, tiled=True)


def swap(value):
    return lax.ppermute(value, "core", [(0, 1), (1, 0)])


def reach(value, hop):
    return lax.ppermute(value, "zl", [(i, i ^ hop) for i in range(lax.axis_size("zl"))])


def call(body, out, *args, flops=0, moved=0, **more):
    return pl.pallas_call(
        body,
        out_shape=out,
        cost_estimate=pl.CostEstimate(flops=flops, bytes_accessed=moved, transcendentals=0),
        compiler_params=pltpu.CompilerParams(vmem_limit_bytes=16 * 2**20),
        **more,
    )(*args)


def far(value):
    return pltpu.with_memory_space_constraint(value, pltpu.HBM)


def shape(dims, kind):
    return jax.ShapeDtypeStruct(dims, kind)


def columns_dot(a, b):
    return lax.dot_general(a, b, (((0,), (0,)), ((), ())), preferred_element_type=F32)


def rows_dot(a, b):
    return lax.dot_general(a, b, (((1,), (1,)), ((), ())), preferred_element_type=F32)


def low_body(x_ref, cot_ref, a_ref, b_ref, mine_ref, theirs_ref):
    acts = rows_dot(x_ref[...], a_ref[...].astype(BF))
    grads = rows_dot(cot_ref[...], b_ref[...].astype(BF))
    both = jnp.concatenate([acts, grads], axis=1)
    half = both.shape[0] // 2
    first = lax.axis_index("core") == 0
    mine_ref[...] = jnp.where(first, both[:half], both[half:])
    theirs_ref[...] = jnp.where(first, both[half:], both[:half])


def pair_body(mine_ref, theirs_ref, out_ref):
    total = (mine_ref[...] + theirs_ref[...]).astype(BF)
    for i in range(out_ref.shape[0]):
        out_ref[i] = total


def stack(value, wide):
    return jnp.concatenate([value[:, i : i + wide] for i in range(0, value.shape[1], wide)], axis=0)


def unstack(value, tall):
    return jnp.concatenate([value[i : i + tall] for i in range(0, value.shape[0], tall)], axis=1)


def gradient_body(scale, x_ref, cot_ref, mine_ref, theirs_ref, out_ref):
    mine, theirs = mine_ref[...].astype(F32), theirs_ref[...].astype(F32)
    first = lax.axis_index("core") == 0
    low = jnp.concatenate([jnp.where(first, mine, theirs), jnp.where(first, theirs, mine)], axis=0)
    rank = low.shape[1] // 2
    low = low.astype(BF)
    count, deep, wide = out_ref.shape
    grad_a = stack(columns_dot(low, x_ref[...])[rank:], wide) * scale
    grad_b = columns_dot(low, cot_ref[...])[:rank] * scale
    rows_a, rows_b = grad_a.shape[0] // count, rank // count
    blank = jnp.zeros((deep - rows_a - rows_b, wide), F32)
    for i in range(count):
        parts = [grad_a[i * rows_a : (i + 1) * rows_a], grad_b[i * rows_b : (i + 1) * rows_b], blank]
        out_ref[i] = jnp.concatenate(parts, axis=0).astype(BF)


def total_of(ref):
    total = ref[0].astype(F32)
    for i in range(1, ref.shape[0]):
        total = total + ref[i].astype(F32)
    return total


def sum_body(in_ref, out_ref):
    total = total_of(in_ref).astype(BF)
    for i in range(out_ref.shape[0]):
        out_ref[i] = total


def shard_body(moment_a_ref, second_a_ref, moment_b_ref, second_b_ref, moment_ref, second_ref):
    deep, wide = moment_ref.shape
    rank = moment_a_ref.shape[0]
    count = lax.axis_size(PLANE)
    rows_a, rows_b = rank * moment_a_ref.shape[1] // wide // count, rank // count
    place = lax.axis_index(PLANE)
    column = pl.multiple_of(place * rows_a // rank * wide, wide)
    row = pl.multiple_of(lax.rem(place * rows_a, rank), rows_a)
    most = max(rows_b, 8)
    row_b = pl.multiple_of(place * rows_b // most * most, most)

    def piece(a_ref, b_ref):
        of_b = b_ref[pl.ds(row_b, most), :]
        chosen = of_b[:rows_b]
        for i in range(rows_b, most, rows_b):
            chosen = jnp.where(place * rows_b == row_b + i, of_b[i : i + rows_b], chosen)
        pad = jnp.ones((deep - rows_a - rows_b, wide), F32)
        return jnp.concatenate([a_ref[pl.ds(row, rows_a), pl.ds(column, wide)], chosen, pad], axis=0)

    moment_ref[...] = piece(moment_a_ref, moment_b_ref)
    second_ref[...] = piece(second_a_ref, second_b_ref)


def adam_body(in_ref, moment_ref, second_ref, out_ref):
    step = adam_step(total_of(in_ref), moment_ref[...], second_ref[...]).astype(BF)
    for i in range(out_ref.shape[0]):
        out_ref[i] = step


def step_of_a(step_ref, rank, width):
    count, _, wide = step_ref.shape
    rows_a = rank * width // wide // count
    step = jnp.concatenate([step_ref[i].astype(F32)[:rows_a] for i in range(count)], axis=0)
    return unstack(step, rank)


def inner_body(step_ref, a_ref, flat_ref, out_ref):
    rank, width = a_ref.shape
    new_a = (a_ref[...] - learn_rate * step_of_a(step_ref, rank, width)).astype(BF)
    inner = rows_dot(new_a, flat_ref[...]).astype(BF)
    for i in range(out_ref.shape[0]):
        out_ref[i] = inner


def step_body(step_ref, b_ref, step_a_ref, step_b_ref, new_b_ref):
    count = step_ref.shape[0]
    rank, width = step_a_ref.shape
    rows_a, rows_b = rank * width // step_ref.shape[2] // count, rank // count
    step_a_ref[...] = step_of_a(step_ref, rank, width)
    parts = [step_ref[i].astype(F32)[rows_a : rows_a + rows_b] for i in range(count)]
    step_b = jnp.concatenate(parts, axis=0)
    step_b_ref[...] = step_b
    new_b_ref[...] = (b_ref[...] - learn_rate * step_b).astype(BF)


def base_body(value_ref, *refs):
    pieces, out_ref, held, value, copied = refs[:4], *refs[4:]
    core, chip = lax.axis_index("core"), lax.axis_index("zl")
    chips = value.shape[0]
    half = chips // 2
    copies = []
    for i in range(chips):
        place = lax.bitwise_xor(chip, i // half + i % half * half)
        for j in range(2):
            copies.append(
                (
                    pltpu.make_async_copy(
                        pieces[2 * j + i // half].at[i % half], held.at[i, j], copied.at[i, j, 0]
                    ),
                    pltpu.make_async_copy(
                        value_ref.at[place, core if j == 0 else 1 - core], value.at[i, j], copied.at[i, j, 1]
                    ),
                )
            )
    for pair in copies:
        for copy in pair:
            copy.start()
    total = jnp.zeros(out_ref.shape, F32)
    for i in range(chips):
        for j in range(2):
            for copy in copies[2 * i + j]:
                copy.wait()
            total += jnp.dot(held[i, j], value[i, j], preferred_element_type=F32)
    out_ref[...] = total


def cache_body(steps, q_ref, k_ref, v_ref, new_ref, length_ref, out_ref, weight_ref):
    groups, wide = length_ref.shape
    tall = q_ref.shape[0] // groups
    heads = q_ref.shape[1] // HD
    slots = wide // (tall // steps)
    row = lax.broadcasted_iota(jnp.int32, (heads * tall, wide), 0) % tall
    column = lax.broadcasted_iota(jnp.int32, (heads * tall, wide), 1)
    same = row // steps == column // slots
    slot = column % slots
    scale = 1.0 / math.sqrt(HD)
    for g in range(groups):
        query = jnp.concatenate(
            [q_ref[g * tall : (g + 1) * tall, h * HD : (h + 1) * HD] for h in range(heads)], axis=0
        )
        old = rows_dot(query, k_ref[g * wide : (g + 1) * wide, :]) * scale
        old = jnp.where(same & (slot < length_ref[g : g + 1, :]), old, -1e30)
        new = rows_dot(query, new_ref[...]) * scale
        token = column - g * tall
        seen = (token >= 0) & (token < tall) & (token // steps == row // steps) & (token <= row)
        new = jnp.where(seen, new, -1e30)
        largest = jnp.maximum(
            jnp.max(old, axis=1, keepdims=True), jnp.max(new, axis=1, keepdims=True)
        )
        old, new = jnp.exp(old - largest), jnp.exp(new - largest)
        total = jnp.sum(old, axis=1, keepdims=True) + jnp.sum(new, axis=1, keepdims=True)
        at = slice(g * heads * tall, (g + 1) * heads * tall)
        weight_ref[at, :] = (new / total).astype(BF)
        out_ref[at, :] = jnp.dot(
            (old / total).astype(BF), v_ref[g * wide : (g + 1) * wide, :], preferred_element_type=F32
        )


def last_body(groups, inner_ref, new_b_ref, base_ref, old_ref, weight_ref, out_ref):
    inner = total_of(inner_ref).astype(BF)
    change = columns_dot(inner, new_b_ref[...])
    values = (base_ref[...] + adapter_scale * change).astype(BF)
    rows, steps, wide = out_ref.shape
    each = rows // groups
    tall = each * steps
    heads = wide // HD
    for g in range(groups):
        at = slice(g * heads * tall, (g + 1) * heads * tall)
        out = old_ref[at, :] + jnp.dot(weight_ref[at, :], values, preferred_element_type=F32)
        for h in range(heads):
            part = out[h * tall : (h + 1) * tall].reshape(each, steps, HD)
            out_ref[g * each : (g + 1) * each, :, h * HD : (h + 1) * HD] = part.astype(BF)


def local(
    trainer_token_input,
    cotangent,
    adapter_a,
    adapter_b,
    moment_a,
    second_a,
    moment_b,
    second_b,
    value_matrix,
    decode_states,
    new_keys,
    queries,
    cache_keys,
    cache_values,
    lengths,
):
    pairs = lax.axis_size("zl")
    tensor = lax.axis_size(TENSOR)
    plane = lax.axis_size(PLANE)
    tokens, width = trainer_token_input.shape
    rank = adapter_a.shape[1]
    kv = cotangent.shape[1]
    rows, steps, _ = decode_states.shape
    count = rows * steps
    slots = cache_keys.shape[1]
    two = 2 * rank
    flat = lax.optimization_barrier(decode_states.reshape(count, width))
    a_turned = adapter_a.T

    half = shape((tokens // 2, two), F32)
    starts = (trainer_token_input, cotangent, a_turned, adapter_b)
    mine, theirs = call(low_body, (half, half), *map(far, starts))
    pair = call(pair_body, shape((pairs, tokens // 2, two), BF), mine, swap(theirs))

    pair, send = lax.optimization_barrier((pair, flat))
    second_chip = reach(send[None], 2)
    mine = jnp.sum(trade(pair, "zl").astype(F32), axis=0).astype(BF)
    mine, moments = lax.optimization_barrier((mine, (moment_a.T, second_a.T, moment_b, second_b)))
    theirs = swap(mine)
    rows_a, rows_b = rank * width // kv // plane, rank // plane
    deep = rows_a + rows_b + -(rows_a + rows_b) % 8
    piece = shape((deep, kv), F32)
    moments = call(shard_body, (piece, piece), *map(far, moments))
    theirs, moments = lax.optimization_barrier((theirs, moments))

    scale = adapter_scale / (tokens * lax.axis_size(DP))
    block = call(
        lambda *refs: gradient_body(scale, *refs),
        shape((plane, deep, kv), BF),
        trainer_token_input,
        cotangent,
        mine,
        theirs,
    )

    block, query = lax.optimization_barrier((block, queries))
    shard = trade(block, PLANE)

    groups = rows * slots // HD
    heads = queries.shape[2] // HD
    old, weights = call(
        lambda *refs: cache_body(steps, *refs),
        (shape((count * heads, HD), F32), shape((count * heads, count), BF)),
        query.reshape(count, heads * HD),
        cache_keys.reshape(rows * slots, kv),
        cache_values.reshape(rows * slots, kv),
        new_keys.reshape(count, kv),
        jnp.repeat(lengths, slots).reshape(groups, HD),
        flops=2 * count * heads * HD * HD * 3,
        moved=8 * 2**20,
    )
    shard, old, weights = lax.optimization_barrier((shard, old, weights))
    near = jnp.concatenate([send[None], second_chip], axis=0)
    distant = reach(near, 1)
    near_other = swap(near)
    shard = call(sum_body, shape((lax.axis_size("zh"), deep, kv), BF), shard)
    shard = trade(shard, "zh")

    step = adam_step(jnp.sum(shard.astype(F32), axis=0), *moments).astype(BF)
    step = jnp.broadcast_to(step[None], (plane, deep, kv))
    distant_sent, _ = lax.optimization_barrier((distant, step))
    distant_other = swap(distant_sent)
    step = trade(step, PLANE)

    inner = call(inner_body, shape((tensor, rank, count), BF), step, a_turned, flat)
    inner = trade(inner, TENSOR)
    step_a, step_b, new_b = call(
        step_body, (shape((rank, width), F32), shape((rank, kv), F32), shape((rank, kv), BF)), step, adapter_b
    )
    base = call(
        base_body,
        shape((count, kv), F32),
        far(value_matrix.reshape(pairs, 2, width, kv)),
        near,
        distant,
        near_other,
        distant_other,
        flops=2 * count * tensor * width * kv,
        moved=4 * 2**20,
        in_specs=[pl.BlockSpec(memory_space=pl.ANY)] * 5,
        scratch_shapes=[
            pltpu.VMEM((pairs, 2, count, width), BF),
            pltpu.VMEM((pairs, 2, width, kv), BF),
            pltpu.SemaphoreType.DMA((pairs, 2, 2)),
        ],
    )

    attended = call(
        lambda *refs: last_body(groups, *refs),
        shape((rows, steps, heads * HD), BF),
        inner,
        new_b,
        base,
        old,
        weights,
    )
    return (step_a.T, step_b, attended)


def solution(mesh):
    sizes = (4, 4, 4, mesh.devices.shape[1] // 2, 2)
    fine = Mesh(mesh.devices.reshape(sizes), DP + TENSOR)
    return jax.shard_map(
        local,
        mesh=fine,
        in_specs=(
            P(DP, TENSOR),
            P(DP, TENSOR),
            P(TENSOR, None),
            P(None, TENSOR),
            P(TENSOR, None),
            P(TENSOR, None),
            P(None, TENSOR),
            P(None, TENSOR),
            P(None, TENSOR),
            P(DP, None, TENSOR),
            P(DP, None, TENSOR),
            P(DP, None, TENSOR),
            P(DP, None, TENSOR),
            P(DP, None, TENSOR),
            P(DP),
        ),
        out_specs=(P(TENSOR, None), P(None, TENSOR), P(DP, None, TENSOR)),
        check_vma=False,
    )
```
